32 devices in a mesh: seq: 16 (over z, y, x), fsdp: 2 (over core).
Axes of the slice: x: 2, y: 2, z: 4, core: 2. Of those that a mesh axis runs over, the one named last changes fastest.
Arguments:
- tokens: bfloat16 [2, 12288, 1024], P('fsdp', 'seq'), may hold values from -6 to 6
- span_flags: int32 [2, 16], P('fsdp', 'seq'), may hold values from 0 to 1, as said below
- norm_gain: bfloat16 [1024], P(('seq', 'fsdp')), may hold values from 0.5 to 1.5
- conv_weight: bfloat16 [3, 1024], P(None, ('seq', 'fsdp')), may hold values from -3.5 to 3.5
- in_weight: bfloat16 [1024, 3072], P(('seq', 'fsdp')), may hold values from -0.1875 to 0.1875
- out_weight: bfloat16 [1024, 1024], P(('seq', 'fsdp')), may hold values from -0.1875 to 0.1875
- ffn_gain: bfloat16 [1024], P(('seq', 'fsdp')), may hold values from 0.5 to 1.5
- gate_weight: bfloat16 [1024, 4608], P(('seq', 'fsdp')), may hold values from -0.1875 to 0.1875
- up_weight: bfloat16 [1024, 4608], P(('seq', 'fsdp')), may hold values from -0.1875 to 0.1875
- down_weight: bfloat16 [4608, 1024], P(('seq', 'fsdp')), may hold values from -0.09375 to 0.09375
- cotangent: bfloat16 [2, 12288, 1024], P('fsdp', 'seq'), may hold values from -6 to 6
Outputs:
- output: bfloat16 [2, 12288, 1024], P('fsdp', 'seq')
- input_grad: float32 [2, 12288, 1024], P('fsdp', 'seq')
- norm_gain_grad: float32 [1024], P(('seq', 'fsdp'))
- conv_weight_grad: float32 [3, 1024], P(None, ('seq', 'fsdp'))
- in_weight_grad: float32 [1024, 3072], P(('seq', 'fsdp'))
- out_weight_grad: float32 [1024, 1024], P(('seq', 'fsdp'))
- ffn_gain_grad: float32 [1024], P(('seq', 'fsdp'))
- gate_weight_grad: float32 [1024, 4608], P(('seq', 'fsdp'))
- up_weight_grad: float32 [1024, 4608], P(('seq', 'fsdp'))
- down_weight_grad: float32 [4608, 1024], P(('seq', 'fsdp'))
The draws below stay inside these ranges and needn't reach their ends.
Inputs may be any that keep to these rules, and one draw needn't show every extreme that they name: span_flags[s, c] is 1 where block c of stream s begins a new sequence; block 0 of every stream begins one and block 1 never does.
All inputs are finite; a program needn't handle non-finite values.
Results may differ from the reference program's by a relative error of at most 0.015.
Values may be sent and summed in bfloat16 or wider, within the bound.
No kernel may reach another device: no remote copies, remote signals or barrier semaphores. Data moves between devices by JAX's collectives and lax.ppermute only.
A program may use at most 256 MiB of HBM per device.

```python
import jax
import jax.numpy as jnp
from jax import lax

D = 1024
FF = 4608
KERNEL = 3
STREAMS = 2
SPANS = 16
STREAM_TOK = 12288


def draw_span_flags(key, part):
    random_bits = jax.random.randint(key, (STREAMS, SPANS), 0, 4)
    starts = (random_bits == 0).astype(jnp.int32)
    column = jnp.arange(SPANS)[None, :]
    starts = jnp.where(column == 0, 1, jnp.where(column == 1, 0, starts))
    return starts.astype(jnp.int32)


def level_of(stream_key, extent, cuts, smallest, largest):
    level, own = 1.0, jax.random.fold_in(stream_key, 6)
    for axis_at, parts in cuts:
        heights = jnp.exp(jax.random.uniform(jax.random.fold_in(own, axis_at), (parts,), jnp.float32, smallest / len(cuts), largest / len(cuts)))
        level = level * jnp.repeat(heights, extent[axis_at] // parts).reshape([-1 if axis == axis_at else 1 for axis in range(len(extent))])
    return level


def noise(stream_key, extent, width, bound, split=(), held_as=jnp.bfloat16):
    loudness = level_of(stream_key, extent, split, -0.22, 0.18) if split else 1.0
    values = jax.random.normal(stream_key, extent, jnp.float32) * width * loudness
    return jnp.minimum(jnp.maximum(values, -bound), bound).astype(held_as)


def setup_inputs(seed: int = 0) -> dict:
    streams_of = jax.random.split(jax.random.key(seed), 12)
    tokens = noise(streams_of[0], (STREAMS, STREAM_TOK, D), 1.0, 6.0, ((0, 2), (1, 16)))
    span_flags = draw_span_flags(jax.random.fold_in(streams_of[11], 71), 0)
    norm_gain = jnp.clip(1.0 + 0.1 * jax.random.normal(streams_of[2], (D,), jnp.float32), 0.5, 1.5).astype(jnp.bfloat16)
    conv_weight = noise(streams_of[3], (KERNEL, D), KERNEL ** -0.5, 3.5, ((1, 32),))
    in_weight = noise(streams_of[4], (D, 3 * D), D ** -0.5, 0.1875, ((0, 32),))
    out_weight = noise(streams_of[5], (D, D), D ** -0.5, 0.1875, ((0, 32),))
    ffn_gain = jnp.clip(1.0 + 0.1 * jax.random.normal(streams_of[6], (D,), jnp.float32), 0.5, 1.5).astype(jnp.bfloat16)
    gate_weight = noise(streams_of[7], (D, FF), D ** -0.5, 0.1875, ((0, 32),))
    up_weight = noise(streams_of[8], (D, FF), D ** -0.5, 0.1875, ((0, 32),))
    down_weight = noise(streams_of[9], (FF, D), FF ** -0.5, 0.09375, ((0, 32),))
    cotangent = noise(streams_of[10], (STREAMS, STREAM_TOK, D), 1.0, 6.0, ((0, 2), (1, 16)))
    return dict(tokens=tokens, span_flags=span_flags, norm_gain=norm_gain, conv_weight=conv_weight, in_weight=in_weight, out_weight=out_weight, ffn_gain=ffn_gain, gate_weight=gate_weight, up_weight=up_weight, down_weight=down_weight, cotangent=cotangent)


EPSILON = 1e-05
HIGHEST = lax.Precision.HIGHEST

@jax.custom_vjp
def low(v):
    return lax.optimization_barrier(v.astype(jnp.bfloat16)).astype(jnp.float32)

@jax.custom_vjp
def low_back(v):
    return v

def low_keep(v):
    return (low(v), None)

def low_pass(kept, grad):
    return (grad,)

def back_keep(v):
    return (v, None)

def back_low(kept, grad):
    return (low(grad),)
low.defvjp(low_keep, low_pass)
low_back.defvjp(back_keep, back_low)

def matmul(left, right):
    return jnp.dot(left, right, precision=HIGHEST, preferred_element_type=jnp.float32)

def rms_scale(values):
    return lax.rsqrt(lax.optimization_barrier(jnp.mean(values * values, axis=-1, keepdims=True)) + EPSILON)

def span_front(weights, inputs):
    norm_gain, conv_weight, in_weight, out_weight, ffn_gain, gate_weight, up_weight, down_weight = weights
    stream_count, row_count, model_width = inputs.shape
    rows_flat = inputs.reshape(-1, model_width)
    hidden = low(rows_flat * rms_scale(rows_flat) * norm_gain)
    projected = low_back(matmul(hidden, in_weight))
    b_part = projected[:, :model_width]
    c_part = projected[:, model_width:2 * model_width]
    v_part = projected[:, 2 * model_width:]
    gated = low(b_part * v_part).reshape(stream_count, row_count, model_width)
    return (gated, c_part.reshape(stream_count, row_count, model_width))

def span_back(weights, inputs, gated, c_part, carried, flag_now):
    norm_gain, conv_weight, in_weight, out_weight, ffn_gain, gate_weight, up_weight, down_weight = weights
    stream_count, row_count, model_width = inputs.shape
    rows_flat = inputs.reshape(-1, model_width)
    keep_state = (1 - flag_now).astype(jnp.float32)[:, None, None]
    extended = jnp.concatenate([carried * keep_state, gated], axis=1)
    conv_out = conv_weight[0] * extended[:, :-2] + conv_weight[1] * extended[:, 1:-1] + conv_weight[2] * extended[:, 2:]
    mixed = low(c_part.reshape(-1, model_width) * conv_out.reshape(-1, model_width))
    resid = rows_flat + low_back(matmul(mixed, out_weight))
    hidden2 = low(resid * rms_scale(resid) * ffn_gain)
    gate_proj = low_back(matmul(hidden2, gate_weight))
    up_proj = low_back(matmul(hidden2, up_weight))
    active = low(jax.nn.silu(gate_proj) * up_proj)
    result = resid + low_back(matmul(active, down_weight))
    return result.reshape(stream_count, row_count, model_width)

def run_block(inputs, weights, span_flags):
    stream_count, total_len, model_width = inputs.shape
    span_count = span_flags.shape[1]
    row_count = total_len // span_count
    blocks = inputs.reshape(stream_count, span_count, row_count, model_width).transpose(1, 0, 2, 3)
    front = jax.checkpoint(span_front)
    back = jax.checkpoint(span_back)

    def front_one(piece):
        return front(weights, piece)
    gated_all, c_all = lax.map(front_one, blocks)
    leading = jnp.zeros((1, stream_count, 2, model_width), jnp.float32)
    carried_all = jnp.concatenate([leading, gated_all[:-1, :, -2:]], axis=0)

    def back_one(pieces):
        piece, gated, c_part, carried, flag_now = pieces
        return back(weights, piece, gated, c_part, carried, flag_now)
    outputs = lax.map(back_one, (blocks, gated_all, c_all, carried_all, span_flags.T))
    return outputs.transpose(1, 0, 2, 3).reshape(stream_count, total_len, model_width)

def reference(tokens, span_flags, norm_gain, conv_weight, in_weight, out_weight, ffn_gain, gate_weight, up_weight, down_weight, cotangent):
    weights = (norm_gain.astype(jnp.float32), conv_weight.astype(jnp.float32), in_weight.astype(jnp.float32), out_weight.astype(jnp.float32), ffn_gain.astype(jnp.float32), gate_weight.astype(jnp.float32), up_weight.astype(jnp.float32), down_weight.astype(jnp.float32))

    def forward(inputs, params):
        return run_block(inputs, params, span_flags)
    result, pullback = jax.vjp(forward, tokens.astype(jnp.float32), weights)
    input_grad, grads = pullback(cotangent.astype(jnp.float32))
    return (result.astype(jnp.bfloat16), input_grad, grads[0], grads[1], grads[2], grads[3], grads[4], grads[5], grads[6], grads[7])
```

```python
import jax
import jax.numpy as jnp
from jax import lax
from jax.sharding import PartitionSpec as P

EPSILON = 1e-05
LANES = 128
BF16 = jnp.bfloat16
F32 = jnp.float32


def swap_cores(x):
    return lax.ppermute(x, "fsdp", [(0, 1), (1, 0)])


def across(x, bit):
    peers = lax.axis_size("seq")
    return lax.ppermute(x, "seq", [(i, i ^ bit) for i in range(peers)])


def shift(x, by):
    peers = lax.axis_size("seq")
    pairs = [(i, i + by) for i in range(peers) if 0 <= i + by < peers]
    return lax.ppermute(x, "seq", pairs)


def columns_of_line(peers):
    return [[4 * z + p for z in range(peers // 4)] for p in range(4)]


def gather_chips(shard):
    peers = lax.axis_size("seq")
    rows, cols = shard.shape
    if peers != 16:
        whole = lax.all_gather(shard, "seq", axis=0, tiled=True)
        return whole.reshape(peers, rows, cols)
    depth = peers // 4
    half = depth // 2
    plane = lax.axis_index("seq") % 4
    line = lax.all_gather(
        shard, "seq", axis_index_groups=columns_of_line(peers), axis=0, tiled=True
    ).reshape(depth, 1, rows, cols)
    from_x = across(line, 1)
    from_y = across(line, 2)
    corner_low = across(from_x[:half], 2)
    corner_high = across(from_y[half:], 1)
    whole = jnp.zeros((depth, 4, rows, cols), shard.dtype)
    whole = lax.dynamic_update_slice(whole, line, (0, plane, 0, 0))
    whole = lax.dynamic_update_slice(whole, from_x, (0, plane ^ 1, 0, 0))
    whole = lax.dynamic_update_slice(whole, from_y, (0, plane ^ 2, 0, 0))
    whole = lax.dynamic_update_slice(whole, corner_low, (0, plane ^ 3, 0, 0))
    whole = lax.dynamic_update_slice(whole, corner_high, (half, plane ^ 3, 0, 0))
    return whole.reshape(peers, rows, cols)


def scatter_chips(terms):
    peers, rows, cols = terms.shape
    if peers != 16:
        flat = terms.reshape(peers * rows, cols)
        return lax.psum_scatter(flat, "seq", scatter_dimension=0, tiled=True)
    depth = peers // 4
    half = depth // 2
    plane = lax.axis_index("seq") % 4
    terms = terms.reshape(depth, 4, rows, cols)

    def piece(bits, start, count):
        return lax.dynamic_slice(
            terms, (start, plane ^ bits, 0, 0), (count, 1, rows, cols)
        )

    add_y = across(piece(3, 0, half), 1)
    add_x = across(piece(3, half, half), 2)
    for_x = jnp.concatenate([piece(1, 0, half), piece(1, half, half) + add_x], axis=0)
    for_y = jnp.concatenate([piece(2, 0, half) + add_y, piece(2, half, half)], axis=0)
    mine = (
        piece(0, 0, depth).astype(F32)
        + across(for_x, 1).astype(F32)
        + across(for_y, 2).astype(F32)
    ).astype(BF16)
    return lax.psum_scatter(
        mine.reshape(depth * rows, cols),
        "seq",
        axis_index_groups=columns_of_line(peers),
        scatter_dimension=0,
        tiled=True,
    )


def rms_scale(values):
    return lax.rsqrt(jnp.mean(values * values, axis=-1, keepdims=True) + EPSILON)


def inner_rows(left, right):
    return lax.dot_general(
        left, right, (((0,), (0,)), ((), ())), preferred_element_type=F32
    )


def times(left, right):
    return jnp.dot(left, right, preferred_element_type=F32)


def times_transposed(left, right):
    return lax.dot_general(
        left, right, (((1,), (1,)), ((), ())), preferred_element_type=F32
    )


def local(
    tokens,
    span_flags,
    norm_gain,
    conv_weight,
    in_weight,
    out_weight,
    ffn_gain,
    gate_weight,
    up_weight,
    down_weight,
    cotangent,
):
    chips = lax.axis_size("seq")
    core = lax.axis_index("fsdp")
    first = core == 0
    rows, width = tokens.shape[1:]
    half = width // 2
    part = in_weight.shape[0]
    pair = 2 * part
    ff_block = down_weight.shape[0]
    ff_half = chips * ff_block

    def ordered(mine, other):
        return jnp.where(first, mine, other), jnp.where(first, other, mine)

    def trade(low, high):
        keep, give = jnp.where(first, low, high), jnp.where(first, high, low)
        return ordered(keep, swap_cores(give))

    tokens_other = swap_cores(tokens[0])
    flag_other = swap_cores(jnp.broadcast_to(span_flags.astype(F32), (8, LANES)))

    in_split = in_weight.reshape(part, 3, 2, half)
    tiny = jnp.concatenate(
        [norm_gain[:, None], ffn_gain[:, None], conv_weight.T], axis=1
    )
    tiny = jnp.pad(tiny, ((0, 0), (0, LANES - tiny.shape[1])))
    in_low = jnp.concatenate([in_split[:, :, 0].reshape(part, 3 * half), tiny], axis=1)
    in_high = jnp.concatenate([in_split[:, :, 1].reshape(part, 3 * half), tiny], axis=1)
    in_pair = jnp.concatenate(trade(in_low, in_high), axis=0)
    out_fold = jnp.concatenate([out_weight[:, :half], out_weight[:, half:]], axis=0)
    front = gather_chips(jnp.concatenate([in_pair, out_fold], axis=1))

    wide = jnp.concatenate([gate_weight, up_weight], axis=1)
    wide = wide.reshape(part, 2 * chips, 2, ff_block)
    wide_low = wide[:, :, 0].reshape(part, 2 * ff_half)
    wide_high = wide[:, :, 1].reshape(part, 2 * ff_half)
    wide_pair = jnp.concatenate(trade(wide_low, wide_high), axis=0)
    weight_gate = gather_chips(wide_pair[:, :ff_half]).reshape(width, ff_half)
    weight_up = gather_chips(wide_pair[:, ff_half:]).reshape(width, ff_half)
    weight_down = gather_chips(down_weight).reshape(ff_half, width)
    cotangent_other = swap_cores(cotangent[0])

    weight_in = front[:, :, : 3 * half].reshape(width, 3 * half)
    small = front[:, :, 3 * half : 3 * half + LANES].reshape(width, LANES)
    small = small[:, :8].astype(F32).T
    gain_first, gain_second = small[0], small[1]
    taps = lax.dynamic_slice(small[2:5], (0, core * half), (3, half))
    out_mine = front[:, :, 3 * half + LANES :]
    out_even, out_odd = ordered(out_mine, swap_cores(out_mine))
    weight_out = jnp.stack(
        [
            jnp.concatenate([out_even[:, :part], out_even[:, part:]], axis=2),
            jnp.concatenate([out_odd[:, :part], out_odd[:, part:]], axis=2),
        ],
        axis=1,
    ).reshape(width, width)

    own_inputs = tokens[0].astype(F32)
    inputs = jnp.concatenate([tokens[0], tokens_other], axis=0).astype(F32)
    keep_state = 1.0 - jnp.stack([span_flags[0, 0].astype(F32), flag_other[0, 0]])
    keep_state = keep_state[:, None, None]
    hidden = (inputs * rms_scale(inputs) * gain_first).astype(BF16)
    projected = times(hidden, weight_in)
    b_part = projected[:, :half]
    c_part = projected[:, half : 2 * half]
    v_part = projected[:, 2 * half :]
    gated = (b_part * v_part).astype(BF16).reshape(2, rows, half)
    incoming = shift(gated[:, -2:], 1)
    extended = jnp.concatenate(
        [incoming.astype(F32) * keep_state, gated.astype(F32)], axis=1
    )
    conv_out = (
        taps[0] * extended[:, :-2] + taps[1] * extended[:, 1:-1] + taps[2] * extended[:, 2:]
    ).reshape(2 * rows, half)
    mixed_half = (c_part * conv_out).astype(BF16)
    mixed = jnp.concatenate(
        ordered(mixed_half[:rows], swap_cores(mixed_half[rows:])), axis=1
    )

    resid = own_inputs + times(mixed, weight_out)
    scale_two = rms_scale(resid)
    normed_two = resid * scale_two
    hidden2_own = (normed_two * gain_second).astype(BF16)
    hidden2 = jnp.concatenate([hidden2_own, swap_cores(hidden2_own)], axis=0)

    gate_proj = times(hidden2, weight_gate)
    up_proj = times(hidden2, weight_up)
    sigmoid_gate = jax.nn.sigmoid(gate_proj)
    silu_gate = gate_proj * sigmoid_gate
    active = (silu_gate * up_proj).astype(BF16)
    result = times(active, weight_down)
    result = resid + result[:rows] + swap_cores(result[rows:].astype(BF16)).astype(F32)
    output = result.astype(BF16)[None]

    d_down = jnp.concatenate([cotangent[0], cotangent_other], axis=0)
    grad_down = inner_rows(active, d_down).astype(BF16)
    shard_down = scatter_chips(grad_down.reshape(chips, ff_block, width))
    d_active = times_transposed(d_down, weight_down)
    d_gate = (
        d_active * up_proj * sigmoid_gate * (1.0 + gate_proj * (1.0 - sigmoid_gate))
    ).astype(BF16)
    d_upper = (d_active * silu_gate).astype(BF16)
    d_hidden2 = times_transposed(d_gate, weight_gate) + times_transposed(d_upper, weight_up)
    d_hidden2 = d_hidden2[:rows] + swap_cores(d_hidden2[rows:])
    grad_gate = inner_rows(hidden2, d_gate).astype(BF16)
    shard_gate = scatter_chips(grad_gate.reshape(chips, pair, ff_half))
    grad_up = inner_rows(hidden2, d_upper).astype(BF16)
    shard_up = scatter_chips(grad_up.reshape(chips, pair, ff_half))

    grad_gain_two = jnp.sum(d_hidden2 * normed_two, axis=0)
    d_normed_two = d_hidden2 * gain_second
    d_resid = cotangent[0].astype(F32) + scale_two * (
        d_normed_two - normed_two * jnp.mean(d_normed_two * normed_two, axis=1, keepdims=True)
    )
    d_branch = d_resid.astype(BF16)
    d_mixed_own = times_transposed(d_branch, weight_out)
    d_mixed_keep = jnp.where(first, d_mixed_own[:, :half], d_mixed_own[:, half:])
    d_mixed_give = jnp.where(first, d_mixed_own[:, half:], d_mixed_own[:, :half])
    d_mixed = jnp.concatenate([d_mixed_keep, swap_cores(d_mixed_give)], axis=0)
    grad_out = inner_rows(mixed, d_branch).reshape(chips, 2, part, width)
    out_keep = jnp.where(first, grad_out[:, 0], grad_out[:, 1])
    out_give = jnp.where(first, grad_out[:, 1], grad_out[:, 0]).astype(BF16)
    grad_out = (out_keep + swap_cores(out_give).astype(F32)).astype(BF16)
    grad_out = jnp.concatenate([grad_out[:, :, :half], grad_out[:, :, half:]], axis=1)

    d_c_part = d_mixed * conv_out
    d_conv = (d_mixed * c_part).reshape(2, rows, half)
    grad_taps = jnp.stack(
        [
            jnp.sum(d_conv * extended[:, :-2], axis=(0, 1)),
            jnp.sum(d_conv * extended[:, 1:-1], axis=(0, 1)),
            jnp.sum(d_conv * extended[:, 2:], axis=(0, 1)),
        ]
    )
    d_state = (
        jnp.concatenate(
            [
                taps[0] * d_conv[:, :1],
                taps[0] * d_conv[:, 1:2] + taps[1] * d_conv[:, :1],
            ],
            axis=1,
        )
        * keep_state
    )
    from_next = shift(d_state, -1)
    following = jnp.pad(d_conv, ((0, 0), (0, 2), (0, 0)))
    d_gated = (
        taps[2] * following[:, :-2] + taps[1] * following[:, 1:-1] + taps[0] * following[:, 2:]
    ) + jnp.pad(from_next, ((0, 0), (rows - 2, 0), (0, 0)))
    d_gated = d_gated.reshape(2 * rows, half)
    d_projected = jnp.concatenate(
        [d_gated * v_part, d_c_part, d_gated * b_part], axis=1
    ).astype(BF16)
    d_hidden = times_transposed(d_projected, weight_in)
    d_hidden = d_hidden[:rows] + swap_cores(d_hidden[rows:])
    grad_in = inner_rows(hidden, d_projected).astype(BF16)

    scale_one = rms_scale(own_inputs)
    normed_one = own_inputs * scale_one
    grad_gain_one = jnp.sum(d_hidden * normed_one, axis=0)
    d_normed_one = d_hidden * gain_first
    input_grad = d_resid + scale_one * (
        d_normed_one - normed_one * jnp.mean(d_normed_one * normed_one, axis=1, keepdims=True)
    )

    zero_half = jnp.zeros_like(grad_taps)
    taps_wide = jnp.concatenate(
        [jnp.where(first, grad_taps, zero_half), jnp.where(first, zero_half, grad_taps)], axis=1
    )
    small_grads = jnp.concatenate([grad_gain_one[None], grad_gain_two[None], taps_wide], axis=0)
    small_grads = jnp.pad(small_grads.T, ((0, 0), (0, LANES - small_grads.shape[0])))
    shard_front = scatter_chips(
        jnp.concatenate(
            [
                grad_in.reshape(chips, pair, 3 * half),
                small_grads.astype(BF16).reshape(chips, pair, LANES),
                grad_out,
            ],
            axis=2,
        )
    )

    def rejoin(shard):
        keep = jnp.where(first, shard[:part], shard[part:])
        give = jnp.where(first, shard[part:], shard[:part])
        return keep, swap_cores(give)

    keep, got = rejoin(shard_front[:, : 3 * half + LANES])
    low, high = ordered(keep[:, : 3 * half], got[:, : 3 * half])
    shard_in = (
        jnp.stack([low.reshape(part, 3, half), high.reshape(part, 3, half)], axis=2)
        .reshape(part, 3 * width)
        .astype(F32)
    )
    tail = keep[:, 3 * half :].astype(F32) + got[:, 3 * half :].astype(F32)
    tail = tail[:, :8].T
    out_pieces = shard_front[:, 3 * half + LANES :]
    shard_out = jnp.concatenate([out_pieces[:part], out_pieces[part:]], axis=1).astype(F32)

    def interleave(shard):
        low, high = ordered(*rejoin(shard))
        return (
            jnp.stack(
                [low.reshape(part, chips, ff_block), high.reshape(part, chips, ff_block)], axis=2
            )
            .reshape(part, 2 * ff_half)
            .astype(F32)
        )

    return (
        output,
        input_grad[None],
        tail[0],
        tail[2:5],
        shard_in,
        shard_out,
        tail[1],
        interleave(shard_gate),
        interleave(shard_up),
        shard_down.astype(F32),
    )


def solution(mesh):
    return jax.shard_map(
        local,
        mesh=mesh,
        in_specs=(
            P("fsdp", "seq", None),
            P("fsdp", "seq"),
            P(("seq", "fsdp")),
            P(None, ("seq", "fsdp")),
            P(("seq", "fsdp"), None),
            P(("seq", "fsdp"), None),
            P(("seq", "fsdp")),
            P(("seq", "fsdp"), None),
            P(("seq", "fsdp"), None),
            P(("seq", "fsdp"), None),
            P("fsdp", "seq", None),
        ),
        out_specs=(
            P("fsdp", "seq", None),
            P("fsdp", "seq", None),
            P(("seq", "fsdp")),
            P(None, ("seq", "fsdp")),
            P(("seq", "fsdp"), None),
            P(("seq", "fsdp"), None),
            P(("seq", "fsdp")),
            P(("seq", "fsdp"), None),
            P(("seq", "fsdp"), None),
            P(("seq", "fsdp"), None),
        ),
        check_vma=False,
    )
```

```python
import jax
import jax.numpy as jnp
from jax import lax
from jax.experimental import pallas as pl
from jax.experimental.pallas import tpu as pltpu
from jax.sharding import PartitionSpec as P

EPSILON = 1e-05
LANES = 128
BF16 = jnp.bfloat16
F32 = jnp.float32


def swap_cores(x):
    return lax.ppermute(x, "fsdp", [(0, 1), (1, 0)])


def across(x, bit):
    peers = lax.axis_size("seq")
    return lax.ppermute(x, "seq", [(i, i ^ bit) for i in range(peers)])


def shift(x, by):
    peers = lax.axis_size("seq")
    pairs = [(i, i + by) for i in range(peers) if 0 <= i + by < peers]
    return lax.ppermute(x, "seq", pairs)


def columns_of_line(peers):
    return [[4 * z + p for z in range(peers // 4)] for p in range(4)]


def after(x, *before):
    return lax.optimization_barrier((x, *before))[0]


def line_gather(shard):
    peers = lax.axis_size("seq")
    rows, cols = shard.shape
    if peers != 16:
        whole = lax.all_gather(shard, "seq", axis=0, tiled=True)
        return whole.reshape(peers // 4, 4, rows, cols)
    return lax.all_gather(
        shard, "seq", axis_index_groups=columns_of_line(peers), axis=0, tiled=True
    ).reshape(peers // 4, 1, rows, cols)


class Plane:
    def __init__(self, line):
        self.line = line
        self.direct = lax.axis_size("seq") != 16
        if self.direct:
            self.from_x = self.from_y = self.low = self.high = line
            return
        self.from_x = across(line, 1)
        self.from_y = across(line, 2)

    def corners(self):
        if self.direct:
            return
        depth, _, rows, _ = self.line.shape
        if depth > 1:
            half = depth // 2
            self.low = across(self.from_x[:half], 2)
            self.high = across(self.from_y[half:], 1)
            self.high_at = (half, 0)
        else:
            half = rows // 32 * 16
            self.low = across(self.from_x[:, :, :half], 2)
            self.high = across(self.from_y[:, :, half:], 1)
            self.high_at = (0, half)

    def place(self, pick=lambda block: block):
        plane = lax.axis_index("seq") % 4
        line = pick(self.line)
        if self.direct:
            return line
        depth, _, rows, cols = line.shape
        whole = jnp.zeros((depth, 4, rows, cols), line.dtype)
        put = lax.dynamic_update_slice
        whole = put(whole, line, (0, plane, 0, 0))
        whole = put(whole, pick(self.from_x), (0, plane ^ 1, 0, 0))
        whole = put(whole, pick(self.from_y), (0, plane ^ 2, 0, 0))
        whole = put(whole, pick(self.low), (0, plane ^ 3, 0, 0))
        deep, row = self.high_at
        return put(whole, pick(self.high), (deep, plane ^ 3, row, 0))


class Scatter:
    def __init__(self, terms):
        self.peers, self.rows, self.cols = terms.shape
        self.depth = self.peers // 4
        self.half = self.depth // 2
        self.terms = terms
        if self.peers == 16:
            self.terms = terms.reshape(self.depth, 4, self.rows, self.cols)

    def piece(self, bits, start, count):
        plane = lax.axis_index("seq") % 4
        return lax.dynamic_slice(
            self.terms, (start, plane ^ bits, 0, 0), (count, 1, self.rows, self.cols)
        )

    def opened(self, x):
        if self.peers != 16:
            return x
        self.sent = [self.piece(3, 0, self.half), self.piece(3, self.half, self.half)]
        *self.sent, x = lax.optimization_barrier((*self.sent, x))
        self.add_y = across(self.sent[0], 1)
        self.add_x = across(self.sent[1], 2)
        return x

    def turned(self, x):
        if self.peers != 16:
            return x
        half, piece = self.half, self.piece
        add_y, add_x, x = lax.optimization_barrier((self.add_y, self.add_x, x))
        for_x = jnp.concatenate([piece(1, 0, half), piece(1, half, half) + add_x], axis=0)
        for_y = jnp.concatenate([piece(2, 0, half) + add_y, piece(2, half, half)], axis=0)
        for_x, for_y, x = lax.optimization_barrier((for_x, for_y, x))
        self.from_x = across(for_x, 1)
        self.from_y = across(for_y, 2)
        return x

    def landed(self, x):
        if self.peers != 16:
            flat = self.terms.reshape(self.peers * self.rows, self.cols)
            self.shard = lax.psum_scatter(flat, "seq", scatter_dimension=0, tiled=True)
            return x
        from_x, from_y, x = lax.optimization_barrier((self.from_x, self.from_y, x))
        mine = (
            self.piece(0, 0, self.depth).astype(F32) + from_x.astype(F32) + from_y.astype(F32)
        ).astype(BF16)
        mine, x = lax.optimization_barrier((mine, x))
        self.shard = lax.psum_scatter(
            mine.reshape(self.depth * self.rows, self.cols),
            "seq",
            axis_index_groups=columns_of_line(self.peers),
            scatter_dimension=0,
            tiled=True,
        )
        return x


def rms_scale(values):
    return lax.rsqrt(jnp.mean(values * values, axis=-1, keepdims=True) + EPSILON)


def inner_rows(left, right):
    return lax.dot_general(
        left, right, (((0,), (0,)), ((), ())), preferred_element_type=F32
    )


def times(left, right):
    return jnp.dot(left, right, preferred_element_type=F32)


def times_transposed(left, right):
    return lax.dot_general(
        left, right, (((1,), (1,)), ((), ())), preferred_element_type=F32
    )


def chunked(rows):
    step = 256 if rows % 256 == 0 else rows
    return [pl.ds(start, step) for start in range(0, rows, step)]


def call(body, grid, ins, outs, args, flops):
    return pl.pallas_call(
        body,
        grid=(grid,),
        in_specs=ins,
        out_specs=[spec for _, spec in outs],
        out_shape=[shape for shape, _ in outs],
        compiler_params=pltpu.CompilerParams(vmem_limit_bytes=44 * 1024 * 1024),
        cost_estimate=pl.CostEstimate(
            flops=flops, bytes_accessed=flops // 500, transcendentals=0
        ),
    )(*args)


def column_tile(cols):
    for tile in (256, 128):
        if cols % tile == 0:
            return tile
    return cols


def held(x):
    return pl.BlockSpec(x.shape, lambda i: (0, 0))


def by_columns(rows, tile):
    return pl.BlockSpec((rows, tile), lambda i: (0, i))


def by_rows(tile, cols):
    return pl.BlockSpec((tile, cols), lambda i: (i, 0))


def gate_kernel(hidden, weight):
    rows, depth = hidden.shape
    cols = weight.shape[1]
    tile = column_tile(cols)

    def body(hidden_ref, weight_ref, gate_ref):
        for part in chunked(rows):
            gate_ref[part, :] = times(hidden_ref[part, :], weight_ref[...]).astype(BF16)

    out = jax.ShapeDtypeStruct((rows, cols), BF16)
    return call(
        body,
        cols // tile,
        [held(hidden), by_columns(depth, tile)],
        [(out, by_columns(rows, tile))],
        (hidden, weight),
        2 * rows * depth * cols,
    )[0]


def active_kernel(hidden, weight, gate):
    rows, depth = hidden.shape
    cols = weight.shape[1]
    tile = column_tile(cols)

    def body(hidden_ref, weight_ref, gate_ref, active_ref, upper_ref):
        for part in chunked(rows):
            upper = times(hidden_ref[part, :], weight_ref[...])
            gate = gate_ref[part, :].astype(F32)
            active_ref[part, :] = (gate * lax.logistic(gate) * upper).astype(BF16)
            upper_ref[part, :] = upper.astype(BF16)

    out = jax.ShapeDtypeStruct((rows, cols), BF16)
    block = by_columns(rows, tile)
    return call(
        body,
        cols // tile,
        [held(hidden), by_columns(depth, tile), block],
        [(out, block), (out, block)],
        (hidden, weight, gate),
        2 * rows * depth * cols,
    )


def split_kernel(d_down, weight, gate, upper):
    rows, depth = d_down.shape
    cols = weight.shape[0]
    tile = column_tile(cols)

    def body(d_down_ref, weight_ref, gate_ref, upper_ref, d_gate_ref, d_upper_ref):
        for part in chunked(rows):
            d_active = times_transposed(d_down_ref[part, :], weight_ref[...])
            gate = gate_ref[part, :].astype(F32)
            sigmoid = lax.logistic(gate)
            silu = gate * sigmoid
            upper = upper_ref[part, :].astype(F32)
            d_gate_ref[part, :] = (
                d_active * upper * (sigmoid + silu * (1.0 - sigmoid))
            ).astype(BF16)
            d_upper_ref[part, :] = (d_active * silu).astype(BF16)

    out = jax.ShapeDtypeStruct((rows, cols), BF16)
    block = by_columns(rows, tile)
    return call(
        body,
        cols // tile,
        [held(d_down), by_rows(tile, depth), block, block],
        [(out, block), (out, block)],
        (d_down, weight, gate, upper),
        2 * rows * depth * cols,
    )


def by_stream(tile, cols, steps):
    return [
        pl.BlockSpec((tile, cols), lambda i: (jnp.minimum(i, steps - 1), 0)),
        pl.BlockSpec((tile, cols), lambda i: (jnp.maximum(i - steps, 0), 0)),
    ]


def rows_kernel(product, lefts, rights, types):
    rows, depth = lefts[0].shape
    cols = rights[0].shape[1] if product is times else rights[0].shape[0]
    tile = column_tile(rows // 2)
    steps = rows // 2 // tile
    count = len(lefts)

    def body(*refs):
        total = product(refs[0][...], refs[count][...])
        for k in range(1, count):
            total += product(refs[k][...], refs[count + k][...])

        @pl.when(pl.program_id(0) < steps)
        def _():
            refs[-2][...] = total.astype(types[0])

        @pl.when(pl.program_id(0) >= steps)
        def _():
            refs[-1][...] = total.astype(types[1])

    shapes = [jax.ShapeDtypeStruct((rows // 2, cols), kind) for kind in types]
    return call(
        body,
        2 * steps,
        [by_rows(tile, depth)] * count + [held(right) for right in rights],
        list(zip(shapes, by_stream(tile, cols, steps))),
        (*lefts, *rights),
        2 * count * rows * depth * cols,
    )


def row_kernel(left, right, product):
    rows, depth = left.shape
    cols = right.shape[1] if product is times else right.shape[0]
    tile = column_tile(rows)

    def body(left_ref, right_ref, out_ref):
        out_ref[...] = product(left_ref[...], right_ref[...])

    out = jax.ShapeDtypeStruct((rows, cols), F32)
    return call(
        body,
        rows // tile,
        [by_rows(tile, depth), held(right)],
        [(out, by_rows(tile, cols))],
        (left, right),
        16 * rows * depth * cols,
    )[0]


def weight_kernel(left, right):
    depth, rows = left.shape
    cols = right.shape[1]
    tile = column_tile(cols)

    def body(left_ref, right_ref, out_ref):
        out_ref[...] = inner_rows(left_ref[...], right_ref[...]).astype(BF16)

    out = jax.ShapeDtypeStruct((rows, cols), BF16)
    return call(
        body,
        cols // tile,
        [held(left), by_columns(depth, tile)],
        [(out, by_columns(rows, tile))],
        (left, right),
        2 * rows * depth * cols,
    )[0]


def weight_rows_kernel(left, right):
    depth, rows = left.shape
    cols = right.shape[1]
    tile = column_tile(rows)

    def body(left_ref, right_ref, out_ref):
        out_ref[...] = inner_rows(left_ref[...], right_ref[...]).astype(BF16)

    out = jax.ShapeDtypeStruct((rows, cols), BF16)
    return call(
        body,
        rows // tile,
        [by_columns(depth, tile), held(right)],
        [(out, by_rows(tile, cols))],
        (left, right),
        2 * rows * depth * cols,
    )[0]


def local(
    tokens,
    span_flags,
    norm_gain,
    conv_weight,
    in_weight,
    out_weight,
    ffn_gain,
    gate_weight,
    up_weight,
    down_weight,
    cotangent,
):
    chips = lax.axis_size("seq")
    core = lax.axis_index("fsdp")
    first = core == 0
    rows, width = tokens.shape[1:]
    half = width // 2
    part = in_weight.shape[0]
    pair = 2 * part
    ff_block = down_weight.shape[0]
    ff_half = chips * ff_block

    def ordered(mine, other):
        return jnp.where(first, mine, other), jnp.where(first, other, mine)

    def trade(low, high):
        keep, give = jnp.where(first, low, high), jnp.where(first, high, low)
        return ordered(keep, swap_cores(give))

    tokens_other = swap_cores(tokens[0])
    flag_other = swap_cores(jnp.broadcast_to(span_flags.astype(F32), (8, LANES)))

    in_split = in_weight.reshape(part, 3, 2, half)
    tiny = jnp.concatenate(
        [norm_gain[:, None], ffn_gain[:, None], conv_weight.T], axis=1
    )
    tiny = jnp.pad(tiny, ((0, 0), (0, LANES - tiny.shape[1])))
    in_low = jnp.concatenate([in_split[:, :, 0].reshape(part, 3 * half), tiny], axis=1)
    in_high = jnp.concatenate([in_split[:, :, 1].reshape(part, 3 * half), tiny], axis=1)
    in_pair = jnp.concatenate(trade(in_low, in_high), axis=0)
    out_fold = jnp.concatenate([out_weight[:, :half], out_weight[:, half:]], axis=0)
    front = jnp.concatenate([in_pair, out_fold], axis=1)

    wide = jnp.concatenate([gate_weight, up_weight], axis=1)
    wide = wide.reshape(part, 2 * chips, 2, ff_block)
    wide_low = wide[:, :, 0].reshape(part, 2 * ff_half)
    wide_high = wide[:, :, 1].reshape(part, 2 * ff_half)
    wide_pair = jnp.concatenate(trade(wide_low, wide_high), axis=0)
    in_wide = 3 * half
    picks = (
        lambda block: block[..., :in_wide],
        lambda block: block[..., in_wide : in_wide + LANES],
        lambda block: block[..., in_wide + LANES :],
    )
    line_front = line_gather(front)
    if chips == 16:
        plane_down = Plane(after(down_weight, front)[None, None])
        plane_down.corners()
        line_front, down_low, down_high = lax.optimization_barrier(
            (line_front, plane_down.low, plane_down.high)
        )
        plane_down.low, plane_down.high = down_low, down_high
    line_gate = line_gather(wide_pair[:, :ff_half])
    line_up = line_gather(wide_pair[:, ff_half:])
    if chips == 16:
        down_plane = plane_down.place().reshape(4 * ff_block, width)
    else:
        down_plane = down_weight
    weight_down = line_gather(after(down_plane, line_gate)).reshape(ff_half, width)
    plane_front = Plane(line_front)
    front_x, front_y, line_gate = lax.optimization_barrier(
        (plane_front.from_x, plane_front.from_y, line_gate)
    )
    plane_front.from_x, plane_front.from_y = front_x, front_y
    plane_front.corners()
    plane_gate = Plane(line_gate)
    low, high = lax.optimization_barrier((plane_front.low, plane_front.high))
    plane_front.low, plane_front.high = low, high
    fronts = [plane_front.place(pick) for pick in picks]
    cotangent_other = swap_cores(after(cotangent[0], tokens_other))

    weight_in = fronts[0].reshape(width, in_wide)
    small = fronts[1].reshape(width, LANES)
    small = small[:, :8].astype(F32).T
    gain_first, gain_second = small[0], small[1]
    taps = lax.dynamic_slice(small[2:5], (0, core * half), (3, half))
    out_mine = fronts[2].reshape(chips, pair, half)
    out_even, out_odd = ordered(out_mine, swap_cores(out_mine))
    weight_out = jnp.stack(
        [
            jnp.concatenate([out_even[:, :part], out_even[:, part:]], axis=2),
            jnp.concatenate([out_odd[:, :part], out_odd[:, part:]], axis=2),
        ],
        axis=1,
    ).reshape(width, width)

    own_inputs = tokens[0].astype(F32)
    inputs = jnp.concatenate([tokens[0], tokens_other], axis=0).astype(F32)
    keep_state = 1.0 - jnp.stack([span_flags[0, 0].astype(F32), flag_other[0, 0]])
    keep_state = keep_state[:, None, None]
    hidden = (inputs * rms_scale(inputs) * gain_first).astype(BF16)
    gate_x, gate_y, line_up, hidden = lax.optimization_barrier(
        (plane_gate.from_x, plane_gate.from_y, line_up, hidden)
    )
    plane_gate.from_x, plane_gate.from_y = gate_x, gate_y
    plane_gate.corners()
    plane_up = Plane(line_up)
    projected = row_kernel(hidden, weight_in, times)
    b_part = projected[:, :half]
    c_part = projected[:, half : 2 * half]
    v_part = projected[:, 2 * half :]
    gated = (b_part * v_part).astype(BF16).reshape(2, rows, half)
    incoming = shift(gated[:, -2:], 1)
    extended = jnp.concatenate(
        [incoming.astype(F32) * keep_state, gated.astype(F32)], axis=1
    )
    conv_out = (
        taps[0] * extended[:, :-2] + taps[1] * extended[:, 1:-1] + taps[2] * extended[:, 2:]
    ).reshape(2 * rows, half)
    mixed_half = (c_part * conv_out).astype(BF16)
    mixed = jnp.concatenate(
        ordered(mixed_half[:rows], swap_cores(mixed_half[rows:])), axis=1
    )

    resid = own_inputs + times(mixed, weight_out)
    scale_two = rms_scale(resid)
    normed_two = resid * scale_two
    hidden2_own = (normed_two * gain_second).astype(BF16)
    hidden2 = jnp.concatenate([hidden2_own, swap_cores(hidden2_own)], axis=0)

    weight_gate = plane_gate.place().reshape(width, ff_half)
    up_x, up_y, hidden2 = lax.optimization_barrier((plane_up.from_x, plane_up.from_y, hidden2))
    plane_up.from_x, plane_up.from_y = up_x, up_y
    gate_proj = gate_kernel(hidden2, weight_gate)
    plane_up.corners()
    weight_up = plane_up.place().reshape(width, ff_half)
    active, up_proj = active_kernel(hidden2, weight_up, gate_proj)

    d_down = jnp.concatenate([cotangent[0], cotangent_other], axis=0)
    grad_down = weight_rows_kernel(active, d_down)
    scatter_down = Scatter(grad_down.reshape(chips, ff_block, width))
    d_down = scatter_down.opened(d_down)
    d_gate, d_upper = split_kernel(d_down, weight_down, gate_proj, up_proj)
    d_gate = scatter_down.turned(d_gate)
    grad_gate = weight_kernel(hidden2, d_gate)
    scatter_gate = Scatter(grad_gate.reshape(chips, pair, ff_half))
    d_gate = scatter_gate.opened(d_gate)
    d_hidden2, d_hidden2_give = rows_kernel(
        times_transposed, (d_gate, d_upper), (weight_gate, weight_up), (F32, F32)
    )
    d_upper, d_hidden2_give = lax.optimization_barrier((d_upper, d_hidden2_give))
    d_hidden2_got = swap_cores(d_hidden2_give)
    d_upper = scatter_down.landed(d_upper)
    grad_up = scatter_gate.turned(weight_kernel(hidden2, d_upper))
    d_hidden2 = d_hidden2 + after(d_hidden2_got, grad_up)

    grad_gain_two = jnp.sum(d_hidden2 * normed_two, axis=0)
    d_normed_two = d_hidden2 * gain_second
    d_resid = cotangent[0].astype(F32) + scale_two * (
        d_normed_two - normed_two * jnp.mean(d_normed_two * normed_two, axis=1, keepdims=True)
    )
    d_branch = d_resid.astype(BF16)
    d_mixed_own = times_transposed(d_branch, weight_out)
    d_mixed_keep = jnp.where(first, d_mixed_own[:, :half], d_mixed_own[:, half:])
    d_mixed_give = jnp.where(first, d_mixed_own[:, half:], d_mixed_own[:, :half])
    d_mixed = jnp.concatenate([d_mixed_keep, swap_cores(d_mixed_give)], axis=0)
    grad_out = inner_rows(mixed, d_branch).reshape(chips, 2, part, width)
    out_keep = jnp.where(first, grad_out[:, 0], grad_out[:, 1])
    out_give = jnp.where(first, grad_out[:, 1], grad_out[:, 0]).astype(BF16)
    grad_out = (out_keep + swap_cores(out_give).astype(F32)).astype(BF16)
    grad_out = jnp.concatenate([grad_out[:, :, :half], grad_out[:, :, half:]], axis=1)

    scatter_up = Scatter(
        jnp.concatenate([grad_up.reshape(chips, pair, ff_half), grad_out], axis=2)
    )
    d_mixed = scatter_up.opened(d_mixed)

    d_c_part = d_mixed * conv_out
    d_conv = (d_mixed * c_part).reshape(2, rows, half)
    grad_taps = jnp.stack(
        [
            jnp.sum(d_conv * extended[:, :-2], axis=(0, 1)),
            jnp.sum(d_conv * extended[:, 1:-1], axis=(0, 1)),
            jnp.sum(d_conv * extended[:, 2:], axis=(0, 1)),
        ]
    )
    d_state = (
        jnp.concatenate(
            [
                taps[0] * d_conv[:, :1],
                taps[0] * d_conv[:, 1:2] + taps[1] * d_conv[:, :1],
            ],
            axis=1,
        )
        * keep_state
    )
    from_next = shift(d_state, -1)
    d_conv = scatter_up.turned(scatter_gate.landed(d_conv))
    following = jnp.pad(d_conv, ((0, 0), (0, 2), (0, 0)))
    d_gated = (
        taps[2] * following[:, :-2] + taps[1] * following[:, 1:-1] + taps[0] * following[:, 2:]
    ) + jnp.pad(from_next, ((0, 0), (rows - 2, 0), (0, 0)))
    d_gated = d_gated.reshape(2 * rows, half)
    d_projected = jnp.concatenate(
        [d_gated * v_part, d_c_part, d_gated * b_part], axis=1
    ).astype(BF16)
    d_hidden, d_hidden_give = rows_kernel(
        times_transposed, (d_projected,), (weight_in,), (F32, F32)
    )
    d_projected = after(d_projected, d_hidden_give)
    grad_in = scatter_up.landed(weight_kernel(hidden, d_projected))
    d_hidden = d_hidden + after(swap_cores(d_hidden_give), grad_in)

    scale_one = rms_scale(own_inputs)
    normed_one = own_inputs * scale_one
    grad_gain_one = jnp.sum(d_hidden * normed_one, axis=0)
    d_normed_one = d_hidden * gain_first
    input_grad = d_resid + scale_one * (
        d_normed_one - normed_one * jnp.mean(d_normed_one * normed_one, axis=1, keepdims=True)
    )

    zero_half = jnp.zeros_like(grad_taps)
    taps_wide = jnp.concatenate(
        [jnp.where(first, grad_taps, zero_half), jnp.where(first, zero_half, grad_taps)], axis=1
    )
    small_grads = jnp.concatenate([grad_gain_one[None], grad_gain_two[None], taps_wide], axis=0)
    small_grads = jnp.pad(small_grads.T, ((0, 0), (0, LANES - small_grads.shape[0])))
    front_terms = jnp.concatenate(
        [
            grad_in.reshape(chips, pair, in_wide),
            small_grads.astype(BF16).reshape(chips, pair, LANES),
        ],
        axis=2,
    )
    scatter_front = Scatter(front_terms)

    result, result_give = rows_kernel(
        times, (scatter_front.opened(active),), (weight_down,), (F32, BF16)
    )
    result_give = scatter_front.turned(result_give)
    result = resid + result + swap_cores(result_give).astype(F32)
    output = scatter_front.landed(result.astype(BF16)[None])
    shard_down, shard_gate, shard_up, output = lax.optimization_barrier(
        (scatter_down.shard, scatter_gate.shard, scatter_up.shard, output)
    )
    shard_front = scatter_front.shard

    def rejoin(shard):
        keep = jnp.where(first, shard[:part], shard[part:])
        give = jnp.where(first, shard[part:], shard[:part])
        return keep, swap_cores(give)

    keep, got = rejoin(shard_front[:, : 3 * half + LANES])
    low, high = ordered(keep[:, : 3 * half], got[:, : 3 * half])
    shard_in = (
        jnp.stack([low.reshape(part, 3, half), high.reshape(part, 3, half)], axis=2)
        .reshape(part, 3 * width)
        .astype(F32)
    )
    tail = keep[:, 3 * half :].astype(F32) + got[:, 3 * half :].astype(F32)
    tail = tail[:, :8].T
    out_pieces = shard_up[:, ff_half:]
    shard_out = jnp.concatenate([out_pieces[:part], out_pieces[part:]], axis=1).astype(F32)

    def interleave(shard):
        low, high = ordered(*rejoin(shard))
        return (
            jnp.stack(
                [low.reshape(part, chips, ff_block), high.reshape(part, chips, ff_block)], axis=2
            )
            .reshape(part, 2 * ff_half)
            .astype(F32)
        )

    return (
        output,
        input_grad[None],
        tail[0],
        tail[2:5],
        shard_in,
        shard_out,
        tail[1],
        interleave(shard_gate),
        interleave(shard_up[:, :ff_half]),
        shard_down.astype(F32),
    )


def solution(mesh):
    return jax.shard_map(
        local,
        mesh=mesh,
        in_specs=(
            P("fsdp", "seq", None),
            P("fsdp", "seq"),
            P(("seq", "fsdp")),
            P(None, ("seq", "fsdp")),
            P(("seq", "fsdp"), None),
            P(("seq", "fsdp"), None),
            P(("seq", "fsdp")),
            P(("seq", "fsdp"), None),
            P(("seq", "fsdp"), None),
            P(("seq", "fsdp"), None),
            P("fsdp", "seq", None),
        ),
        out_specs=(
            P("fsdp", "seq", None),
            P("fsdp", "seq", None),
            P(("seq", "fsdp")),
            P(None, ("seq", "fsdp")),
            P(("seq", "fsdp"), None),
            P(("seq", "fsdp"), None),
            P(("seq", "fsdp")),
            P(("seq", "fsdp"), None),
            P(("seq", "fsdp"), None),
            P(("seq", "fsdp"), None),
        ),
        check_vma=False,
    )
```

```python
import jax
import jax.numpy as jnp
from jax import lax
from jax.experimental import pallas as pl
from jax.experimental.pallas import tpu as pltpu
from jax.sharding import PartitionSpec as P

EPSILON = 1e-05
LANES = 128
BF16 = jnp.bfloat16
F32 = jnp.float32


def swap_cores(x):
    return lax.ppermute(x, "fsdp", [(0, 1), (1, 0)])


def across(x, bit):
    peers = lax.axis_size("seq")
    return lax.ppermute(x, "seq", [(i, i ^ bit) for i in range(peers)])


def shift(x, by):
    peers = lax.axis_size("seq")
    pairs = [(i, i + by) for i in range(peers) if 0 <= i + by < peers]
    return lax.ppermute(x, "seq", pairs)


def columns_of_line(peers):
    return [[4 * z + p for z in range(peers // 4)] for p in range(4)]


def after(x, *before):
    return lax.optimization_barrier((x, *before))[0]


def line_gather(shard):
    peers = lax.axis_size("seq")
    rows, cols = shard.shape
    if peers != 16:
        whole = lax.all_gather(shard, "seq", axis=0, tiled=True)
        return whole.reshape(peers // 4, 4, rows, cols)
    return lax.all_gather(
        shard, "seq", axis_index_groups=columns_of_line(peers), axis=0, tiled=True
    ).reshape(peers // 4, 1, rows, cols)


class Plane:
    def __init__(self, line):
        self.line = line
        self.direct = lax.axis_size("seq") != 16
        if self.direct:
            self.from_x = self.from_y = self.low = self.high = line
            return
        self.from_x = across(line, 1)
        self.from_y = across(line, 2)

    def corners(self):
        if self.direct:
            return
        depth, _, rows, _ = self.line.shape
        if depth > 1:
            half = depth // 2
            self.low = across(self.from_x[:half], 2)
            self.high = across(self.from_y[half:], 1)
            self.high_at = (half, 0)
        else:
            half = rows // 32 * 16
            self.low = across(self.from_x[:, :, :half], 2)
            self.high = across(self.from_y[:, :, half:], 1)
            self.high_at = (0, half)

    def place(self, pick=lambda block: block):
        plane = lax.axis_index("seq") % 4
        line = pick(self.line)
        if self.direct:
            return line
        depth, _, rows, cols = line.shape
        whole = jnp.zeros((depth, 4, rows, cols), line.dtype)
        put = lax.dynamic_update_slice
        whole = put(whole, line, (0, plane, 0, 0))
        whole = put(whole, pick(self.from_x), (0, plane ^ 1, 0, 0))
        whole = put(whole, pick(self.from_y), (0, plane ^ 2, 0, 0))
        whole = put(whole, pick(self.low), (0, plane ^ 3, 0, 0))
        deep, row = self.high_at
        return put(whole, pick(self.high), (deep, plane ^ 3, row, 0))


class Scatter:
    def __init__(self, terms):
        self.peers, self.rows, self.cols = terms.shape
        self.depth = self.peers // 4
        self.half = self.depth // 2
        self.terms = terms
        if self.peers == 16:
            self.terms = terms.reshape(self.depth, 4, self.rows, self.cols)

    def piece(self, bits, start, count):
        plane = lax.axis_index("seq") % 4
        return lax.dynamic_slice(
            self.terms, (start, plane ^ bits, 0, 0), (count, 1, self.rows, self.cols)
        )

    def opened(self, x):
        if self.peers != 16:
            return x
        self.sent = [self.piece(3, 0, self.half), self.piece(3, self.half, self.half)]
        *self.sent, x = lax.optimization_barrier((*self.sent, x))
        self.add_y = across(self.sent[0], 1)
        self.add_x = across(self.sent[1], 2)
        return x

    def turned(self, x):
        if self.peers != 16:
            return x
        half, piece = self.half, self.piece
        add_y, add_x, x = lax.optimization_barrier((self.add_y, self.add_x, x))
        for_x = jnp.concatenate([piece(1, 0, half), piece(1, half, half) + add_x], axis=0)
        for_y = jnp.concatenate([piece(2, 0, half) + add_y, piece(2, half, half)], axis=0)
        for_x, for_y, x = lax.optimization_barrier((for_x, for_y, x))
        self.from_x = across(for_x, 1)
        self.from_y = across(for_y, 2)
        return x

    def landed(self, x):
        if self.peers != 16:
            flat = self.terms.reshape(self.peers * self.rows, self.cols)
            self.shard = lax.psum_scatter(flat, "seq", scatter_dimension=0, tiled=True)
            return x
        from_x, from_y, x = lax.optimization_barrier((self.from_x, self.from_y, x))
        mine = (
            self.piece(0, 0, self.depth).astype(F32) + from_x.astype(F32) + from_y.astype(F32)
        ).astype(BF16)
        mine, x = lax.optimization_barrier((mine, x))
        self.shard = lax.psum_scatter(
            mine.reshape(self.depth * self.rows, self.cols),
            "seq",
            axis_index_groups=columns_of_line(self.peers),
            scatter_dimension=0,
            tiled=True,
        )
        return x


def rms_scale(values):
    return lax.rsqrt(jnp.mean(values * values, axis=-1, keepdims=True) + EPSILON)


def inner_rows(left, right):
    return lax.dot_general(
        left, right, (((0,), (0,)), ((), ())), preferred_element_type=F32
    )


def times(left, right):
    return jnp.dot(left, right, preferred_element_type=F32)


def times_transposed(left, right):
    return lax.dot_general(
        left, right, (((1,), (1,)), ((), ())), preferred_element_type=F32
    )


def chunked(rows):
    step = 256 if rows % 256 == 0 else rows
    return [pl.ds(start, step) for start in range(0, rows, step)]


def call(body, grid, ins, outs, args, flops):
    return pl.pallas_call(
        body,
        grid=(grid,),
        in_specs=ins,
        out_specs=[spec for _, spec in outs],
        out_shape=[shape for shape, _ in outs],
        compiler_params=pltpu.CompilerParams(vmem_limit_bytes=44 * 1024 * 1024),
        cost_estimate=pl.CostEstimate(
            flops=flops, bytes_accessed=flops // 500, transcendentals=0
        ),
    )(*args)


def column_tile(cols):
    for tile in (256, 128):
        if cols % tile == 0:
            return tile
    return cols


def held(x):
    return pl.BlockSpec(x.shape, lambda i: (0, 0))


def by_columns(rows, tile):
    return pl.BlockSpec((rows, tile), lambda i: (0, i))


def by_rows(tile, cols):
    return pl.BlockSpec((tile, cols), lambda i: (i, 0))


def gate_kernel(hidden, weight):
    rows, depth = hidden.shape
    cols = weight.shape[1]
    tile = column_tile(cols)

    def body(hidden_ref, weight_ref, gate_ref):
        for part in chunked(rows):
            gate_ref[part, :] = times(hidden_ref[part, :], weight_ref[...]).astype(BF16)

    out = jax.ShapeDtypeStruct((rows, cols), BF16)
    return call(
        body,
        cols // tile,
        [held(hidden), by_columns(depth, tile)],
        [(out, by_columns(rows, tile))],
        (hidden, weight),
        2 * rows * depth * cols,
    )[0]


def active_kernel(hidden, weight, gate):
    rows, depth = hidden.shape
    cols = weight.shape[1]
    tile = column_tile(cols)

    def body(hidden_ref, weight_ref, gate_ref, active_ref, upper_ref):
        for part in chunked(rows):
            upper = times(hidden_ref[part, :], weight_ref[...])
            gate = gate_ref[part, :].astype(F32)
            active_ref[part, :] = (gate * lax.logistic(gate) * upper).astype(BF16)
            upper_ref[part, :] = upper.astype(BF16)

    out = jax.ShapeDtypeStruct((rows, cols), BF16)
    block = by_columns(rows, tile)
    return call(
        body,
        cols // tile,
        [held(hidden), by_columns(depth, tile), block],
        [(out, block), (out, block)],
        (hidden, weight, gate),
        2 * rows * depth * cols,
    )


def split_kernel(d_down, weight, gate, upper):
    rows, depth = d_down.shape
    cols = weight.shape[0]
    tile = column_tile(cols)

    def body(d_down_ref, weight_ref, gate_ref, upper_ref, d_gate_ref, d_upper_ref):
        for part in chunked(rows):
            d_active = times_transposed(d_down_ref[part, :], weight_ref[...])
            gate = gate_ref[part, :].astype(F32)
            sigmoid = lax.logistic(gate)
            silu = gate * sigmoid
            upper = upper_ref[part, :].astype(F32)
            d_gate_ref[part, :] = (
                d_active * upper * (sigmoid + silu * (1.0 - sigmoid))
            ).astype(BF16)
            d_upper_ref[part, :] = (d_active * silu).astype(BF16)

    out = jax.ShapeDtypeStruct((rows, cols), BF16)
    block = by_columns(rows, tile)
    return call(
        body,
        cols // tile,
        [held(d_down), by_rows(tile, depth), block, block],
        [(out, block), (out, block)],
        (d_down, weight, gate, upper),
        2 * rows * depth * cols,
    )


def by_stream(tile, cols, steps):
    return [
        pl.BlockSpec((tile, cols), lambda i: (jnp.minimum(i, steps - 1), 0)),
        pl.BlockSpec((tile, cols), lambda i: (jnp.maximum(i - steps, 0), 0)),
    ]


def rows_kernel(product, lefts, rights, types):
    rows, depth = lefts[0].shape
    cols = rights[0].shape[1] if product is times else rights[0].shape[0]
    tile = column_tile(rows // 2)
    steps = rows // 2 // tile
    count = len(lefts)

    def body(*refs):
        total = product(refs[0][...], refs[count][...])
        for k in range(1, count):
            total += product(refs[k][...], refs[count + k][...])

        @pl.when(pl.program_id(0) < steps)
        def _():
            refs[-2][...] = total.astype(types[0])

        @pl.when(pl.program_id(0) >= steps)
        def _():
            refs[-1][...] = total.astype(types[1])

    shapes = [jax.ShapeDtypeStruct((rows // 2, cols), kind) for kind in types]
    return call(
        body,
        2 * steps,
        [by_rows(tile, depth)] * count + [held(right) for right in rights],
        list(zip(shapes, by_stream(tile, cols, steps))),
        (*lefts, *rights),
        2 * count * rows * depth * cols,
    )


def row_kernel(left, right, product):
    rows, depth = left.shape
    cols = right.shape[1] if product is times else right.shape[0]
    tile = column_tile(rows)

    def body(left_ref, right_ref, out_ref):
        out_ref[...] = product(left_ref[...], right_ref[...])

    out = jax.ShapeDtypeStruct((rows, cols), F32)
    return call(
        body,
        rows // tile,
        [by_rows(tile, depth), held(right)],
        [(out, by_rows(tile, cols))],
        (left, right),
        16 * rows * depth * cols,
    )[0]


def weight_kernel(left, right):
    depth, rows = left.shape
    cols = right.shape[1]
    tile = column_tile(cols)

    def body(left_ref, right_ref, out_ref):
        out_ref[...] = inner_rows(left_ref[...], right_ref[...]).astype(BF16)

    out = jax.ShapeDtypeStruct((rows, cols), BF16)
    return call(
        body,
        cols // tile,
        [held(left), by_columns(depth, tile)],
        [(out, by_columns(rows, tile))],
        (left, right),
        2 * rows * depth * cols,
    )[0]


def weight_rows_kernel(left, right):
    depth, rows = left.shape
    cols = right.shape[1]
    tile = column_tile(rows)

    def body(left_ref, right_ref, out_ref):
        out_ref[...] = inner_rows(left_ref[...], right_ref[...]).astype(BF16)

    out = jax.ShapeDtypeStruct((rows, cols), BF16)
    return call(
        body,
        rows // tile,
        [by_columns(depth, tile), held(right)],
        [(out, by_rows(tile, cols))],
        (left, right),
        2 * rows * depth * cols,
    )[0]


def local(
    tokens,
    span_flags,
    norm_gain,
    conv_weight,
    in_weight,
    out_weight,
    ffn_gain,
    gate_weight,
    up_weight,
    down_weight,
    cotangent,
):
    chips = lax.axis_size("seq")
    core = lax.axis_index("fsdp")
    first = core == 0
    rows, width = tokens.shape[1:]
    half = width // 2
    part = in_weight.shape[0]
    pair = 2 * part
    ff_block = down_weight.shape[0]
    ff_half = chips * ff_block

    def ordered(mine, other):
        return jnp.where(first, mine, other), jnp.where(first, other, mine)

    def trade(low, high):
        keep, give = jnp.where(first, low, high), jnp.where(first, high, low)
        return ordered(keep, swap_cores(give))

    tokens_other = swap_cores(tokens[0])
    flag_other = swap_cores(jnp.broadcast_to(span_flags.astype(F32), (8, LANES)))

    in_split = in_weight.reshape(part, 3, 2, half)
    tiny = jnp.concatenate(
        [norm_gain[:, None], ffn_gain[:, None], conv_weight.T], axis=1
    )
    tiny = jnp.pad(tiny, ((0, 0), (0, LANES - tiny.shape[1])))
    in_low = jnp.concatenate([in_split[:, :, 0].reshape(part, 3 * half), tiny], axis=1)
    in_high = jnp.concatenate([in_split[:, :, 1].reshape(part, 3 * half), tiny], axis=1)
    in_pair = jnp.concatenate(trade(in_low, in_high), axis=0)
    out_fold = jnp.concatenate([out_weight[:, :half], out_weight[:, half:]], axis=0)
    front = jnp.concatenate([in_pair, out_fold], axis=1)

    gate_weight, up_weight, front = lax.optimization_barrier((gate_weight, up_weight, front))
    wide = jnp.concatenate([gate_weight, up_weight], axis=1)
    wide = wide.reshape(part, 2 * chips, 2, ff_block)
    wide_low = wide[:, :, 0].reshape(part, 2 * ff_half)
    wide_high = wide[:, :, 1].reshape(part, 2 * ff_half)
    wide_pair = jnp.concatenate(trade(wide_low, wide_high), axis=0)
    in_wide = 3 * half
    picks = (
        lambda block: block[..., :in_wide],
        lambda block: block[..., in_wide : in_wide + LANES],
        lambda block: block[..., in_wide + LANES :],
    )
    line_front = line_gather(front)
    if chips == 16:
        plane_down = Plane(after(down_weight, front)[None, None])
        plane_down.corners()
        line_front, down_low, down_high = lax.optimization_barrier(
            (line_front, plane_down.low, plane_down.high)
        )
        plane_down.low, plane_down.high = down_low, down_high
    line_gate = line_gather(wide_pair[:, :ff_half])
    line_up = line_gather(wide_pair[:, ff_half:])
    if chips == 16:
        down_plane = plane_down.place().reshape(4 * ff_block, width)
    else:
        down_plane = down_weight
    weight_down = line_gather(after(down_plane, line_gate)).reshape(ff_half, width)
    plane_front = Plane(line_front)
    front_x, front_y, line_gate = lax.optimization_barrier(
        (plane_front.from_x, plane_front.from_y, line_gate)
    )
    plane_front.from_x, plane_front.from_y = front_x, front_y
    plane_front.corners()
    plane_gate = Plane(line_gate)
    low, high = lax.optimization_barrier((plane_front.low, plane_front.high))
    plane_front.low, plane_front.high = low, high
    fronts = [plane_front.place(pick) for pick in picks]
    cotangent_other = swap_cores(after(cotangent[0], tokens_other))

    weight_in = fronts[0].reshape(width, in_wide)
    small = fronts[1].reshape(width, LANES)
    small = small[:, :8].astype(F32).T
    gain_first, gain_second = small[0], small[1]
    taps = lax.dynamic_slice(small[2:5], (0, core * half), (3, half))
    out_mine = fronts[2].reshape(chips, pair, half)
    out_even, out_odd = ordered(out_mine, swap_cores(out_mine))
    weight_out = jnp.stack(
        [
            jnp.concatenate([out_even[:, :part], out_even[:, part:]], axis=2),
            jnp.concatenate([out_odd[:, :part], out_odd[:, part:]], axis=2),
        ],
        axis=1,
    ).reshape(width, width)

    own_inputs = tokens[0].astype(F32)
    inputs = jnp.concatenate([tokens[0], tokens_other], axis=0).astype(F32)
    keep_state = 1.0 - jnp.stack([span_flags[0, 0].astype(F32), flag_other[0, 0]])
    keep_state = keep_state[:, None, None]
    hidden = (inputs * rms_scale(inputs) * gain_first).astype(BF16)
    gate_x, gate_y, line_up, hidden = lax.optimization_barrier(
        (plane_gate.from_x, plane_gate.from_y, line_up, hidden)
    )
    plane_gate.from_x, plane_gate.from_y = gate_x, gate_y
    plane_gate.corners()
    plane_up = Plane(line_up)
    projected = row_kernel(hidden, weight_in, times)
    b_part = projected[:, :half]
    c_part = projected[:, half : 2 * half]
    v_part = projected[:, 2 * half :]
    gated = (b_part * v_part).astype(BF16).reshape(2, rows, half)
    incoming = shift(gated[:, -2:], 1)
    extended = jnp.concatenate(
        [incoming.astype(F32) * keep_state, gated.astype(F32)], axis=1
    )
    conv_out = (
        taps[0] * extended[:, :-2] + taps[1] * extended[:, 1:-1] + taps[2] * extended[:, 2:]
    ).reshape(2 * rows, half)
    mixed_half = (c_part * conv_out).astype(BF16)
    mixed = jnp.concatenate(
        ordered(mixed_half[:rows], swap_cores(mixed_half[rows:])), axis=1
    )
    up_x, up_y, mixed = lax.optimization_barrier((plane_up.from_x, plane_up.from_y, mixed))
    plane_up.from_x, plane_up.from_y = up_x, up_y
    plane_up.corners()

    resid = own_inputs + times(mixed, weight_out)
    scale_two = rms_scale(resid)
    normed_two = resid * scale_two
    hidden2_own = (normed_two * gain_second).astype(BF16)
    hidden2 = jnp.concatenate([hidden2_own, swap_cores(hidden2_own)], axis=0)

    weight_gate = plane_gate.place().reshape(width, ff_half)
    gate_proj = gate_kernel(hidden2, weight_gate)
    weight_up = plane_up.place().reshape(width, ff_half)
    active, up_proj = active_kernel(hidden2, weight_up, gate_proj)

    d_down = jnp.concatenate([cotangent[0], cotangent_other], axis=0)
    grad_down = weight_rows_kernel(active, d_down)
    scatter_down = Scatter(grad_down.reshape(chips, ff_block, width))
    d_down = scatter_down.opened(d_down)
    d_gate, d_upper = split_kernel(d_down, weight_down, gate_proj, up_proj)
    d_gate = scatter_down.turned(d_gate)
    grad_gate = weight_kernel(hidden2, d_gate)
    scatter_gate = Scatter(grad_gate.reshape(chips, pair, ff_half))
    d_gate = scatter_gate.opened(d_gate)
    d_hidden2, d_hidden2_give = rows_kernel(
        times_transposed, (d_gate, d_upper), (weight_gate, weight_up), (F32, F32)
    )
    d_upper, d_hidden2_give = lax.optimization_barrier((d_upper, d_hidden2_give))
    d_hidden2_got = swap_cores(d_hidden2_give)
    d_upper = scatter_down.landed(d_upper)
    grad_up = scatter_gate.turned(weight_kernel(hidden2, d_upper))
    d_hidden2 = d_hidden2 + after(d_hidden2_got, grad_up)

    grad_gain_two = jnp.sum(d_hidden2 * normed_two, axis=0)
    d_normed_two = d_hidden2 * gain_second
    d_resid = cotangent[0].astype(F32) + scale_two * (
        d_normed_two - normed_two * jnp.mean(d_normed_two * normed_two, axis=1, keepdims=True)
    )
    d_branch = d_resid.astype(BF16)
    d_mixed_own = times_transposed(d_branch, weight_out)
    d_mixed_keep = jnp.where(first, d_mixed_own[:, :half], d_mixed_own[:, half:])
    d_mixed_give = jnp.where(first, d_mixed_own[:, half:], d_mixed_own[:, :half])
    d_mixed = jnp.concatenate([d_mixed_keep, swap_cores(d_mixed_give)], axis=0)
    grad_out = inner_rows(mixed, d_branch).reshape(chips, 2, part, width)
    out_keep = jnp.where(first, grad_out[:, 0], grad_out[:, 1])
    out_give = jnp.where(first, grad_out[:, 1], grad_out[:, 0]).astype(BF16)
    grad_out = (out_keep + swap_cores(out_give).astype(F32)).astype(BF16)
    grad_out = jnp.concatenate([grad_out[:, :, :half], grad_out[:, :, half:]], axis=1)

    scatter_up = Scatter(
        jnp.concatenate([grad_up.reshape(chips, pair, ff_half), grad_out], axis=2)
    )
    d_mixed = scatter_up.opened(d_mixed)

    d_c_part = d_mixed * conv_out
    d_conv = (d_mixed * c_part).reshape(2, rows, half)
    grad_taps = jnp.stack(
        [
            jnp.sum(d_conv * extended[:, :-2], axis=(0, 1)),
            jnp.sum(d_conv * extended[:, 1:-1], axis=(0, 1)),
            jnp.sum(d_conv * extended[:, 2:], axis=(0, 1)),
        ]
    )
    d_state = (
        jnp.concatenate(
            [
                taps[0] * d_conv[:, :1],
                taps[0] * d_conv[:, 1:2] + taps[1] * d_conv[:, :1],
            ],
            axis=1,
        )
        * keep_state
    )
    from_next = shift(d_state, -1)
    d_conv = scatter_gate.landed(d_conv)
    following = jnp.pad(d_conv, ((0, 0), (0, 2), (0, 0)))
    d_gated = (
        taps[2] * following[:, :-2] + taps[1] * following[:, 1:-1] + taps[0] * following[:, 2:]
    ) + jnp.pad(from_next, ((0, 0), (rows - 2, 0), (0, 0)))
    d_gated = d_gated.reshape(2 * rows, half)
    d_projected = jnp.concatenate(
        [d_gated * v_part, d_c_part, d_gated * b_part], axis=1
    ).astype(BF16)
    d_projected = scatter_up.turned(d_projected)
    d_hidden, d_hidden_give = rows_kernel(
        times_transposed, (d_projected,), (weight_in,), (F32, F32)
    )
    d_projected = after(d_projected, d_hidden_give)
    grad_in = weight_kernel(hidden, d_projected)
    d_hidden = d_hidden + after(swap_cores(d_hidden_give), grad_in)

    scale_one = rms_scale(own_inputs)
    normed_one = own_inputs * scale_one
    grad_gain_one = jnp.sum(d_hidden * normed_one, axis=0)
    d_normed_one = d_hidden * gain_first
    input_grad = d_resid + scale_one * (
        d_normed_one - normed_one * jnp.mean(d_normed_one * normed_one, axis=1, keepdims=True)
    )

    zero_half = jnp.zeros_like(grad_taps)
    taps_wide = jnp.concatenate(
        [jnp.where(first, grad_taps, zero_half), jnp.where(first, zero_half, grad_taps)], axis=1
    )
    small_grads = jnp.concatenate([grad_gain_one[None], grad_gain_two[None], taps_wide], axis=0)
    small_grads = jnp.pad(small_grads.T, ((0, 0), (0, LANES - small_grads.shape[0])))
    front_terms = jnp.concatenate(
        [
            grad_in.reshape(chips, pair, in_wide),
            small_grads.astype(BF16).reshape(chips, pair, LANES),
        ],
        axis=2,
    )
    scatter_front = Scatter(front_terms)

    result, result_give = rows_kernel(
        times, (scatter_front.opened(active),), (weight_down,), (F32, BF16)
    )
    result_give = scatter_front.turned(scatter_up.landed(result_give))
    result = resid + result + swap_cores(result_give).astype(F32)
    output = scatter_front.landed(result.astype(BF16)[None])
    shard_down, shard_gate, shard_up, output = lax.optimization_barrier(
        (scatter_down.shard, scatter_gate.shard, scatter_up.shard, output)
    )
    shard_front = scatter_front.shard

    def rejoin(shard):
        keep = jnp.where(first, shard[:part], shard[part:])
        give = jnp.where(first, shard[part:], shard[:part])
        return keep, swap_cores(give)

    keep, got = rejoin(shard_front[:, : 3 * half + LANES])
    low, high = ordered(keep[:, : 3 * half], got[:, : 3 * half])
    shard_in = (
        jnp.stack([low.reshape(part, 3, half), high.reshape(part, 3, half)], axis=2)
        .reshape(part, 3 * width)
        .astype(F32)
    )
    tail = keep[:, 3 * half :].astype(F32) + got[:, 3 * half :].astype(F32)
    tail = tail[:, :8].T
    out_pieces = shard_up[:, ff_half:]
    shard_out = jnp.concatenate([out_pieces[:part], out_pieces[part:]], axis=1).astype(F32)

    def interleave(shard):
        low, high = ordered(*rejoin(shard))
        return (
            jnp.stack(
                [low.reshape(part, chips, ff_block), high.reshape(part, chips, ff_block)], axis=2
            )
            .reshape(part, 2 * ff_half)
            .astype(F32)
        )

    return (
        output,
        input_grad[None],
        tail[0],
        tail[2:5],
        shard_in,
        shard_out,
        tail[1],
        interleave(shard_gate),
        interleave(shard_up[:, :ff_half]),
        shard_down.astype(F32),
    )


def solution(mesh):
    return jax.shard_map(
        local,
        mesh=mesh,
        in_specs=(
            P("fsdp", "seq", None),
            P("fsdp", "seq"),
            P(("seq", "fsdp")),
            P(None, ("seq", "fsdp")),
            P(("seq", "fsdp"), None),
            P(("seq", "fsdp"), None),
            P(("seq", "fsdp")),
            P(("seq", "fsdp"), None),
            P(("seq", "fsdp"), None),
            P(("seq", "fsdp"), None),
            P("fsdp", "seq", None),
        ),
        out_specs=(
            P("fsdp", "seq", None),
            P("fsdp", "seq", None),
            P(("seq", "fsdp")),
            P(None, ("seq", "fsdp")),
            P(("seq", "fsdp"), None),
            P(("seq", "fsdp"), None),
            P(("seq", "fsdp")),
            P(("seq", "fsdp"), None),
            P(("seq", "fsdp"), None),
            P(("seq", "fsdp"), None),
        ),
        check_vma=False,
    )
```

```python
import jax
import jax.numpy as jnp
from jax import lax
from jax.experimental import pallas as pl
from jax.experimental.pallas import tpu as pltpu
from jax.sharding import PartitionSpec as P

EPSILON = 1e-05
LANES = 128
BF16 = jnp.bfloat16
F32 = jnp.float32


def swap_cores(x):
    return lax.ppermute(x, "fsdp", [(0, 1), (1, 0)])


def across(x, bit):
    peers = lax.axis_size("seq")
    return lax.ppermute(x, "seq", [(i, i ^ bit) for i in range(peers)])


def shift(x, by):
    peers = lax.axis_size("seq")
    pairs = [(i, i + by) for i in range(peers) if 0 <= i + by < peers]
    return lax.ppermute(x, "seq", pairs)


def columns_of_line(peers):
    return [[4 * z + p for z in range(peers // 4)] for p in range(4)]


def after(x, *before):
    return lax.optimization_barrier((x, *before))[0]


def line_gather(shard):
    peers = lax.axis_size("seq")
    rows, cols = shard.shape
    if peers != 16:
        whole = lax.all_gather(shard, "seq", axis=0, tiled=True)
        return whole.reshape(peers // 4, 4, rows, cols)
    return lax.all_gather(
        shard, "seq", axis_index_groups=columns_of_line(peers), axis=0, tiled=True
    ).reshape(peers // 4, 1, rows, cols)


class Plane:
    def __init__(self, line):
        self.line = line
        self.direct = lax.axis_size("seq") != 16
        if self.direct:
            self.from_x = self.from_y = self.low = self.high = line
            return
        self.from_x = across(line, 1)
        self.from_y = across(line, 2)

    def corners(self):
        if self.direct:
            return
        depth, _, rows, _ = self.line.shape
        if depth > 1:
            half = depth // 2
            self.low = across(self.from_x[:half], 2)
            self.high = across(self.from_y[half:], 1)
            self.high_at = (half, 0)
        else:
            half = rows // 32 * 16
            self.low = across(self.from_x[:, :, :half], 2)
            self.high = across(self.from_y[:, :, half:], 1)
            self.high_at = (0, half)

    def place(self, pick=lambda block: block):
        plane = lax.axis_index("seq") % 4
        line = pick(self.line)
        if self.direct:
            return line
        depth, _, rows, cols = line.shape
        whole = jnp.zeros((depth, 4, rows, cols), line.dtype)
        put = lax.dynamic_update_slice
        whole = put(whole, line, (0, plane, 0, 0))
        whole = put(whole, pick(self.from_x), (0, plane ^ 1, 0, 0))
        whole = put(whole, pick(self.from_y), (0, plane ^ 2, 0, 0))
        whole = put(whole, pick(self.low), (0, plane ^ 3, 0, 0))
        deep, row = self.high_at
        return put(whole, pick(self.high), (deep, plane ^ 3, row, 0))


class Scatter:
    def __init__(self, terms):
        self.peers, self.rows, self.cols = terms.shape
        self.depth = self.peers // 4
        self.half = self.depth // 2
        self.terms = terms
        if self.peers == 16:
            self.terms = terms.reshape(self.depth, 4, self.rows, self.cols)

    def piece(self, bits, start, count):
        plane = lax.axis_index("seq") % 4
        return lax.dynamic_slice(
            self.terms, (start, plane ^ bits, 0, 0), (count, 1, self.rows, self.cols)
        )

    def opened(self, x):
        if self.peers != 16:
            return x
        self.sent = [self.piece(3, 0, self.half), self.piece(3, self.half, self.half)]
        *self.sent, x = lax.optimization_barrier((*self.sent, x))
        self.add_y = across(self.sent[0], 1)
        self.add_x = across(self.sent[1], 2)
        return x

    def turned(self, x):
        if self.peers != 16:
            return x
        half, piece = self.half, self.piece
        add_y, add_x, x = lax.optimization_barrier((self.add_y, self.add_x, x))
        for_x = jnp.concatenate([piece(1, 0, half), piece(1, half, half) + add_x], axis=0)
        for_y = jnp.concatenate([piece(2, 0, half) + add_y, piece(2, half, half)], axis=0)
        for_x, for_y, x = lax.optimization_barrier((for_x, for_y, x))
        self.from_x = across(for_x, 1)
        self.from_y = across(for_y, 2)
        return x

    def landed(self, x):
        if self.peers != 16:
            flat = self.terms.reshape(self.peers * self.rows, self.cols)
            self.shard = lax.psum_scatter(flat, "seq", scatter_dimension=0, tiled=True)
            return x
        from_x, from_y, x = lax.optimization_barrier((self.from_x, self.from_y, x))
        mine = (
            self.piece(0, 0, self.depth).astype(F32) + from_x.astype(F32) + from_y.astype(F32)
        ).astype(BF16)
        mine, x = lax.optimization_barrier((mine, x))
        self.shard = lax.psum_scatter(
            mine.reshape(self.depth * self.rows, self.cols),
            "seq",
            axis_index_groups=columns_of_line(self.peers),
            scatter_dimension=0,
            tiled=True,
        )
        return x


def rms_scale(values):
    return lax.rsqrt(jnp.mean(values * values, axis=-1, keepdims=True) + EPSILON)


def inner_rows(left, right):
    return lax.dot_general(
        left, right, (((0,), (0,)), ((), ())), preferred_element_type=F32
    )


def times(left, right):
    return jnp.dot(left, right, preferred_element_type=F32)


def times_transposed(left, right):
    return lax.dot_general(
        left, right, (((1,), (1,)), ((), ())), preferred_element_type=F32
    )


def chunked(rows):
    step = 256 if rows % 256 == 0 else rows
    return [pl.ds(start, step) for start in range(0, rows, step)]


def call(body, grid, ins, outs, args, flops):
    return pl.pallas_call(
        body,
        grid=(grid,),
        in_specs=ins,
        out_specs=[spec for _, spec in outs],
        out_shape=[shape for shape, _ in outs],
        compiler_params=pltpu.CompilerParams(vmem_limit_bytes=32 * 1024 * 1024),
        cost_estimate=pl.CostEstimate(
            flops=flops, bytes_accessed=flops // 500, transcendentals=0
        ),
    )(*args)


def column_tile(cols):
    for tile in (256, 128):
        if cols % tile == 0:
            return tile
    return cols


def held(x):
    return pl.BlockSpec(x.shape, lambda i: (0, 0))


def by_columns(rows, tile):
    return pl.BlockSpec((rows, tile), lambda i: (0, i))


def by_rows(tile, cols):
    return pl.BlockSpec((tile, cols), lambda i: (i, 0))


def gate_kernel(hidden, weight):
    rows, depth = hidden.shape
    cols = weight.shape[1]
    tile = column_tile(cols)

    def body(hidden_ref, weight_ref, gate_ref):
        for part in chunked(rows):
            gate_ref[part, :] = times(hidden_ref[part, :], weight_ref[...]).astype(BF16)

    out = jax.ShapeDtypeStruct((rows, cols), BF16)
    return call(
        body,
        cols // tile,
        [held(hidden), by_columns(depth, tile)],
        [(out, by_columns(rows, tile))],
        (hidden, weight),
        2 * rows * depth * cols,
    )[0]


def active_kernel(hidden, weight, gate):
    rows, depth = hidden.shape
    cols = weight.shape[1]
    tile = column_tile(cols)

    def body(hidden_ref, weight_ref, gate_ref, active_ref, upper_ref):
        for part in chunked(rows):
            upper = times(hidden_ref[part, :], weight_ref[...])
            gate = gate_ref[part, :].astype(F32)
            active_ref[part, :] = (gate * lax.logistic(gate) * upper).astype(BF16)
            upper_ref[part, :] = upper.astype(BF16)

    out = jax.ShapeDtypeStruct((rows, cols), BF16)
    block = by_columns(rows, tile)
    return call(
        body,
        cols // tile,
        [held(hidden), by_columns(depth, tile), block],
        [(out, block), (out, block)],
        (hidden, weight, gate),
        2 * rows * depth * cols,
    )


def split_kernel(d_down, weight, gate, upper):
    rows, depth = d_down.shape
    cols = weight.shape[0]
    tile = column_tile(cols)

    def body(d_down_ref, weight_ref, gate_ref, upper_ref, d_gate_ref, d_upper_ref):
        for part in chunked(rows):
            d_active = times_transposed(d_down_ref[part, :], weight_ref[...])
            gate = gate_ref[part, :].astype(F32)
            sigmoid = lax.logistic(gate)
            silu = gate * sigmoid
            upper = upper_ref[part, :].astype(F32)
            d_gate_ref[part, :] = (
                d_active * upper * (sigmoid + silu * (1.0 - sigmoid))
            ).astype(BF16)
            d_upper_ref[part, :] = (d_active * silu).astype(BF16)

    out = jax.ShapeDtypeStruct((rows, cols), BF16)
    block = by_columns(rows, tile)
    return call(
        body,
        cols // tile,
        [held(d_down), by_rows(tile, depth), block, block],
        [(out, block), (out, block)],
        (d_down, weight, gate, upper),
        2 * rows * depth * cols,
    )


def by_stream(tile, cols, steps):
    return [
        pl.BlockSpec((tile, cols), lambda i: (jnp.minimum(i, steps - 1), 0)),
        pl.BlockSpec((tile, cols), lambda i: (jnp.maximum(i - steps, 0), 0)),
    ]


def rows_kernel(product, lefts, rights, types):
    rows, depth = lefts[0].shape
    cols = rights[0].shape[1] if product is times else rights[0].shape[0]
    tile = column_tile(rows // 2)
    steps = rows // 2 // tile
    count = len(lefts)

    def body(*refs):
        total = product(refs[0][...], refs[count][...])
        for k in range(1, count):
            total += product(refs[k][...], refs[count + k][...])

        @pl.when(pl.program_id(0) < steps)
        def _():
            refs[-2][...] = total.astype(types[0])

        @pl.when(pl.program_id(0) >= steps)
        def _():
            refs[-1][...] = total.astype(types[1])

    shapes = [jax.ShapeDtypeStruct((rows // 2, cols), kind) for kind in types]
    return call(
        body,
        2 * steps,
        [by_rows(tile, depth)] * count + [held(right) for right in rights],
        list(zip(shapes, by_stream(tile, cols, steps))),
        (*lefts, *rights),
        2 * count * rows * depth * cols,
    )


def row_kernel(left, right, product):
    rows, depth = left.shape
    cols = right.shape[1] if product is times else right.shape[0]
    tile = column_tile(rows)

    def body(left_ref, right_ref, out_ref):
        out_ref[...] = product(left_ref[...], right_ref[...])

    out = jax.ShapeDtypeStruct((rows, cols), F32)
    return call(
        body,
        rows // tile,
        [by_rows(tile, depth), held(right)],
        [(out, by_rows(tile, cols))],
        (left, right),
        16 * rows * depth * cols,
    )[0]


def weight_kernel(left, right):
    depth, rows = left.shape
    cols = right.shape[1]
    tile = column_tile(cols)

    def body(left_ref, right_ref, out_ref):
        out_ref[...] = inner_rows(left_ref[...], right_ref[...]).astype(BF16)

    out = jax.ShapeDtypeStruct((rows, cols), BF16)
    return call(
        body,
        cols // tile,
        [held(left), by_columns(depth, tile)],
        [(out, by_columns(rows, tile))],
        (left, right),
        2 * rows * depth * cols,
    )[0]


def weight_rows_kernel(left, right):
    depth, rows = left.shape
    cols = right.shape[1]
    tile = column_tile(rows)

    def body(left_ref, right_ref, out_ref):
        out_ref[...] = inner_rows(left_ref[...], right_ref[...]).astype(BF16)

    out = jax.ShapeDtypeStruct((rows, cols), BF16)
    return call(
        body,
        rows // tile,
        [by_columns(depth, tile), held(right)],
        [(out, by_rows(tile, cols))],
        (left, right),
        2 * rows * depth * cols,
    )[0]


def local(
    tokens,
    span_flags,
    norm_gain,
    conv_weight,
    in_weight,
    out_weight,
    ffn_gain,
    gate_weight,
    up_weight,
    down_weight,
    cotangent,
):
    chips = lax.axis_size("seq")
    core = lax.axis_index("fsdp")
    first = core == 0
    rows, width = tokens.shape[1:]
    half = width // 2
    part = in_weight.shape[0]
    pair = 2 * part
    ff_block = down_weight.shape[0]
    ff_half = chips * ff_block

    def ordered(mine, other):
        return jnp.where(first, mine, other), jnp.where(first, other, mine)

    def trade(low, high):
        keep, give = jnp.where(first, low, high), jnp.where(first, high, low)
        return ordered(keep, swap_cores(give))

    tokens_other = swap_cores(tokens[0])
    flag_other = swap_cores(jnp.broadcast_to(span_flags.astype(F32), (8, LANES)))

    in_split = in_weight.reshape(part, 3, 2, half)
    tiny = jnp.concatenate(
        [norm_gain[:, None], ffn_gain[:, None], conv_weight.T], axis=1
    )
    tiny = jnp.pad(tiny, ((0, 0), (0, LANES - tiny.shape[1])))
    in_low = jnp.concatenate([in_split[:, :, 0].reshape(part, 3 * half), tiny], axis=1)
    in_high = jnp.concatenate([in_split[:, :, 1].reshape(part, 3 * half), tiny], axis=1)
    in_pair = jnp.concatenate(trade(in_low, in_high), axis=0)
    out_fold = jnp.concatenate([out_weight[:, :half], out_weight[:, half:]], axis=0)
    front = jnp.concatenate([in_pair, out_fold], axis=1)

    gate_weight, up_weight, front = lax.optimization_barrier((gate_weight, up_weight, front))
    wide = jnp.concatenate([gate_weight, up_weight], axis=1)
    wide = wide.reshape(part, 2 * chips, 2, ff_block)
    wide_low = wide[:, :, 0].reshape(part, 2 * ff_half)
    wide_high = wide[:, :, 1].reshape(part, 2 * ff_half)
    wide_pair = jnp.concatenate(trade(wide_low, wide_high), axis=0)
    in_wide = 3 * half
    picks = (
        lambda block: block[..., :in_wide],
        lambda block: block[..., in_wide : in_wide + LANES],
        lambda block: block[..., in_wide + LANES :],
    )
    line_front = line_gather(front)
    if chips == 16:
        plane_down = Plane(after(down_weight, front)[None, None])
        plane_down.corners()
        line_front, down_low, down_high = lax.optimization_barrier(
            (line_front, plane_down.low, plane_down.high)
        )
        plane_down.low, plane_down.high = down_low, down_high
    line_gate = line_gather(wide_pair[:, :ff_half])
    line_up = line_gather(wide_pair[:, ff_half:])
    if chips == 16:
        down_plane = plane_down.place().reshape(4 * ff_block, width)
    else:
        down_plane = down_weight
    weight_down = line_gather(after(down_plane, line_gate)).reshape(ff_half, width)
    plane_front = Plane(line_front)
    front_x, front_y, line_gate = lax.optimization_barrier(
        (plane_front.from_x, plane_front.from_y, line_gate)
    )
    plane_front.from_x, plane_front.from_y = front_x, front_y
    plane_front.corners()
    plane_gate = Plane(line_gate)
    low, high = lax.optimization_barrier((plane_front.low, plane_front.high))
    plane_front.low, plane_front.high = low, high
    fronts = [plane_front.place(pick) for pick in picks]
    cotangent_other = swap_cores(after(cotangent[0], tokens_other))

    weight_in = fronts[0].reshape(width, in_wide)
    small = fronts[1].reshape(width, LANES)
    small = small[:, :8].astype(F32).T
    gain_first, gain_second = small[0], small[1]
    taps = lax.dynamic_slice(small[2:5], (0, core * half), (3, half))
    out_mine = fronts[2].reshape(chips, pair, half)
    out_even, out_odd = ordered(out_mine, swap_cores(out_mine))
    weight_out = jnp.stack(
        [
            jnp.concatenate([out_even[:, :part], out_even[:, part:]], axis=2),
            jnp.concatenate([out_odd[:, :part], out_odd[:, part:]], axis=2),
        ],
        axis=1,
    ).reshape(width, width)

    own_inputs = tokens[0].astype(F32)
    inputs = jnp.concatenate([tokens[0], tokens_other], axis=0).astype(F32)
    keep_state = 1.0 - jnp.stack([span_flags[0, 0].astype(F32), flag_other[0, 0]])
    keep_state = keep_state[:, None, None]
    hidden = (inputs * rms_scale(inputs) * gain_first).astype(BF16)
    gate_x, gate_y, line_up, hidden = lax.optimization_barrier(
        (plane_gate.from_x, plane_gate.from_y, line_up, hidden)
    )
    plane_gate.from_x, plane_gate.from_y = gate_x, gate_y
    plane_gate.corners()
    plane_up = Plane(line_up)
    projected = row_kernel(hidden, weight_in, times)
    b_part = projected[:, :half]
    c_part = projected[:, half : 2 * half]
    v_part = projected[:, 2 * half :]
    gated = (b_part * v_part).astype(BF16).reshape(2, rows, half)
    incoming = shift(gated[:, -2:], 1)
    extended = jnp.concatenate(
        [incoming.astype(F32) * keep_state, gated.astype(F32)], axis=1
    )
    conv_out = (
        taps[0] * extended[:, :-2] + taps[1] * extended[:, 1:-1] + taps[2] * extended[:, 2:]
    ).reshape(2 * rows, half)
    mixed_half = (c_part * conv_out).astype(BF16)
    mixed = jnp.concatenate(
        ordered(mixed_half[:rows], swap_cores(mixed_half[rows:])), axis=1
    )
    up_x, up_y, mixed = lax.optimization_barrier((plane_up.from_x, plane_up.from_y, mixed))
    plane_up.from_x, plane_up.from_y = up_x, up_y
    plane_up.corners()

    resid = own_inputs + times(mixed, weight_out)
    scale_two = rms_scale(resid)
    normed_two = resid * scale_two
    hidden2_own = (normed_two * gain_second).astype(BF16)
    hidden2 = jnp.concatenate([hidden2_own, swap_cores(hidden2_own)], axis=0)

    weight_gate = plane_gate.place().reshape(width, ff_half)
    gate_proj = gate_kernel(hidden2, weight_gate)
    weight_up = plane_up.place().reshape(width, ff_half)
    active, up_proj = active_kernel(hidden2, weight_up, gate_proj)

    d_down = jnp.concatenate([cotangent[0], cotangent_other], axis=0)
    grad_down = weight_rows_kernel(active, d_down)
    scatter_down = Scatter(grad_down.reshape(chips, ff_block, width))
    d_down = scatter_down.opened(d_down)
    d_gate, d_upper = split_kernel(d_down, weight_down, gate_proj, up_proj)
    d_gate = scatter_down.turned(d_gate)
    grad_gate = weight_kernel(hidden2, d_gate)
    scatter_gate = Scatter(grad_gate.reshape(chips, pair, ff_half))
    d_gate = scatter_gate.opened(d_gate)
    d_hidden2, d_hidden2_give = rows_kernel(
        times_transposed, (d_gate, d_upper), (weight_gate, weight_up), (F32, F32)
    )
    d_upper, d_hidden2_give = lax.optimization_barrier((d_upper, d_hidden2_give))
    d_hidden2_got = swap_cores(d_hidden2_give)
    d_upper = scatter_down.landed(d_upper)
    grad_up = scatter_gate.turned(weight_kernel(hidden2, d_upper))
    d_hidden2 = d_hidden2 + after(d_hidden2_got, grad_up)

    grad_gain_two = jnp.sum(d_hidden2 * normed_two, axis=0)
    d_normed_two = d_hidden2 * gain_second
    d_resid = cotangent[0].astype(F32) + scale_two * (
        d_normed_two - normed_two * jnp.mean(d_normed_two * normed_two, axis=1, keepdims=True)
    )
    d_branch = d_resid.astype(BF16)
    d_mixed_own = times_transposed(d_branch, weight_out)
    d_mixed_keep = jnp.where(first, d_mixed_own[:, :half], d_mixed_own[:, half:])
    d_mixed_give = jnp.where(first, d_mixed_own[:, half:], d_mixed_own[:, :half])
    d_mixed = jnp.concatenate([d_mixed_keep, swap_cores(d_mixed_give)], axis=0)
    grad_out = inner_rows(mixed, d_branch).reshape(chips, 2, part, width)
    out_keep = jnp.where(first, grad_out[:, 0], grad_out[:, 1])
    out_give = jnp.where(first, grad_out[:, 1], grad_out[:, 0]).astype(BF16)
    grad_out = (out_keep + swap_cores(out_give).astype(F32)).astype(BF16)
    grad_out = jnp.concatenate([grad_out[:, :, :half], grad_out[:, :, half:]], axis=1)

    scatter_up = Scatter(
        jnp.concatenate([grad_up.reshape(chips, pair, ff_half), grad_out], axis=2)
    )
    d_mixed = scatter_up.opened(d_mixed)

    d_c_part = d_mixed * conv_out
    d_conv = (d_mixed * c_part).reshape(2, rows, half)
    grad_taps = jnp.stack(
        [
            jnp.sum(d_conv * extended[:, :-2], axis=(0, 1)),
            jnp.sum(d_conv * extended[:, 1:-1], axis=(0, 1)),
            jnp.sum(d_conv * extended[:, 2:], axis=(0, 1)),
        ]
    )
    d_state = (
        jnp.concatenate(
            [
                taps[0] * d_conv[:, :1],
                taps[0] * d_conv[:, 1:2] + taps[1] * d_conv[:, :1],
            ],
            axis=1,
        )
        * keep_state
    )
    from_next = shift(d_state, -1)
    d_conv = scatter_gate.landed(d_conv)
    following = jnp.pad(d_conv, ((0, 0), (0, 2), (0, 0)))
    d_gated = (
        taps[2] * following[:, :-2] + taps[1] * following[:, 1:-1] + taps[0] * following[:, 2:]
    ) + jnp.pad(from_next, ((0, 0), (rows - 2, 0), (0, 0)))
    d_gated = d_gated.reshape(2 * rows, half)
    d_projected = jnp.concatenate(
        [d_gated * v_part, d_c_part, d_gated * b_part], axis=1
    ).astype(BF16)
    d_projected = scatter_up.turned(d_projected)
    d_hidden, d_hidden_give = rows_kernel(
        times_transposed, (d_projected,), (weight_in,), (F32, F32)
    )
    d_projected = after(d_projected, d_hidden_give)
    grad_in = weight_kernel(hidden, d_projected)
    d_hidden = d_hidden + after(swap_cores(d_hidden_give), grad_in)

    scale_one = rms_scale(own_inputs)
    normed_one = own_inputs * scale_one
    grad_gain_one = jnp.sum(d_hidden * normed_one, axis=0)
    d_normed_one = d_hidden * gain_first
    input_grad = d_resid + scale_one * (
        d_normed_one - normed_one * jnp.mean(d_normed_one * normed_one, axis=1, keepdims=True)
    )

    zero_half = jnp.zeros_like(grad_taps)
    taps_wide = jnp.concatenate(
        [jnp.where(first, grad_taps, zero_half), jnp.where(first, zero_half, grad_taps)], axis=1
    )
    small_grads = jnp.concatenate([grad_gain_one[None], grad_gain_two[None], taps_wide], axis=0)
    small_grads = jnp.pad(small_grads.T, ((0, 0), (0, LANES - small_grads.shape[0])))
    front_terms = jnp.concatenate(
        [
            grad_in.reshape(chips, pair, in_wide),
            small_grads.astype(BF16).reshape(chips, pair, LANES),
        ],
        axis=2,
    )
    scatter_front = Scatter(front_terms)

    result, result_give = rows_kernel(
        times, (scatter_front.opened(active),), (weight_down,), (F32, BF16)
    )
    result_give = scatter_front.turned(scatter_up.landed(result_give))
    result = resid + result + swap_cores(result_give).astype(F32)
    output = scatter_front.landed(result.astype(BF16)[None])
    shard_down, shard_gate, shard_up, output = lax.optimization_barrier(
        (scatter_down.shard, scatter_gate.shard, scatter_up.shard, output)
    )
    shard_front = scatter_front.shard

    def rejoin(shard):
        keep = jnp.where(first, shard[:part], shard[part:])
        give = jnp.where(first, shard[part:], shard[:part])
        return keep, swap_cores(give)

    keep, got = rejoin(shard_front[:, : 3 * half + LANES])
    low, high = ordered(keep[:, : 3 * half], got[:, : 3 * half])
    shard_in = (
        jnp.stack([low.reshape(part, 3, half), high.reshape(part, 3, half)], axis=2)
        .reshape(part, 3 * width)
        .astype(F32)
    )
    tail = keep[:, 3 * half :].astype(F32) + got[:, 3 * half :].astype(F32)
    tail = tail[:, :8].T
    out_pieces = shard_up[:, ff_half:]
    shard_out = jnp.concatenate([out_pieces[:part], out_pieces[part:]], axis=1).astype(F32)

    def interleave(shard):
        low, high = ordered(*rejoin(shard))
        return (
            jnp.stack(
                [low.reshape(part, chips, ff_block), high.reshape(part, chips, ff_block)], axis=2
            )
            .reshape(part, 2 * ff_half)
            .astype(F32)
        )

    return (
        output,
        input_grad[None],
        tail[0],
        tail[2:5],
        shard_in,
        shard_out,
        tail[1],
        interleave(shard_gate),
        interleave(shard_up[:, :ff_half]),
        shard_down.astype(F32),
    )


def solution(mesh):
    return jax.shard_map(
        local,
        mesh=mesh,
        in_specs=(
            P("fsdp", "seq", None),
            P("fsdp", "seq"),
            P(("seq", "fsdp")),
            P(None, ("seq", "fsdp")),
            P(("seq", "fsdp"), None),
            P(("seq", "fsdp"), None),
            P(("seq", "fsdp")),
            P(("seq", "fsdp"), None),
            P(("seq", "fsdp"), None),
            P(("seq", "fsdp"), None),
            P("fsdp", "seq", None),
        ),
        out_specs=(
            P("fsdp", "seq", None),
            P("fsdp", "seq", None),
            P(("seq", "fsdp")),
            P(None, ("seq", "fsdp")),
            P(("seq", "fsdp"), None),
            P(("seq", "fsdp"), None),
            P(("seq", "fsdp")),
            P(("seq", "fsdp"), None),
            P(("seq", "fsdp"), None),
            P(("seq", "fsdp"), None),
        ),
        check_vma=False,
    )
```
